128 devices in a mesh: query: 8 (over y, core), index: 16 (over z, x).
Axes of the slice: x: 4, y: 4, z: 4, core: 2. Of those that a mesh axis runs over, the one named last changes fastest.
Arguments:
- tokens: bfloat16 [131072, 768], P(('query', 'index')), may hold values from -24 to 24
- w_in: bfloat16 [768, 3072], replicated, may hold values from -0.21875 to 0.21875
- bias_in: float32 [3072], replicated, may hold values from -3 to 3
- w_out: bfloat16 [3072, 768], replicated, may hold values from -0.109375 to 0.109375
- bias_out: float32 [768], replicated, may hold values from -3 to 3
- gain: float32 [768], replicated, may hold values from 0.5 to 1.5
- shift: float32 [768], replicated, may hold values from -0.5 to 0.5
- slab: bfloat16 [65536, 768], P('index')
- owners: int32 [2048, 64, 1], P(('query', 'index')), may hold values from 0 to 15; in each aligned block of 1024 rows (0 to 1023, 1024 to 2047, ..., all dimensions but the last counted through in order) at most 192 rows name the same one
- offsets: int32 [2048, 64], P(('query', 'index')), may hold values from 0 to 4095
- reader_weights: float32 [2048, 64], P(('query', 'index')), may hold values from 0.01 to 1
Outputs:
- token_grads: bfloat16 [131072, 768], P(('query', 'index'))
- layer_grads: float32 [3072, 1536], P(('query', 'index'))
The draws below stay inside these ranges and needn't reach their ends.
Inputs may be any that keep to these rules, and one draw needn't show every extreme that they name: `owners`: among the rows of one device, no shard number appears more than 192 times, and some shard appears exactly 192 times.
All inputs are finite; a program needn't handle non-finite values.
Results may differ from the reference program's by a relative error of at most 0.0082.
Values may be sent and summed in bfloat16 or wider, within the bound.
No kernel may reach another device: no remote copies, remote signals or barrier semaphores. Data moves between devices by JAX's collectives and lax.ppermute only.
A program may use at most 192 MiB of HBM per device.

```python
import math
import jax
import jax.numpy as jnp
import numpy as np
from jax import lax

D = 768
FF = 3072
LEN = 64
TOPK = 64
Q_DEV = 16
P_DEV = 4096
QUESTIONS = 2048
TOKENS = 131072
CAP = 192
N_QUERY = 8
N_INDEX = 16


def draw_slab(key, part):
    key = jax.random.fold_in(key, 11)
    first = jax.random.fold_in(key, 0)
    shape = (P_DEV * N_INDEX, D)
    base = jnp.clip(jax.random.normal(first, shape, jnp.float32), -6.0, 6.0)
    return base.astype(jnp.bfloat16)


def set_ends(values, rng, least, top_value):
    longest = values.shape.index(max(values.shape))
    spots = []
    for shift in (0, 1):
        where = [jax.random.randint(jax.random.fold_in(rng, axis), (), 0, length) for axis, length in enumerate(values.shape)]
        where[longest] = (where[longest] + shift) % values.shape[longest]
        spots.append(tuple(where))
    return values.at[spots[0]].set(least).at[spots[1]].set(top_value)


def strengthened(entries, rng, source, target, parts, factor):
    def block_of(position):
        return (jnp.arange(entries.shape[position]) // (entries.shape[position] // parts)).reshape((-1,) + (1,) * (entries.ndim - 1 - position))

    first = jax.random.permutation(rng, parts)[block_of(target)]
    second = (block_of(target) + parts // 2) % parts
    return jnp.where((block_of(source) == first) | (block_of(source) == second), factor * entries, entries)


def block_levels(stream_key, extent, cuts, least, top_value):
    level, own = 1.0, jax.random.fold_in(stream_key, 6)
    for dim, parts in cuts:
        heights = jnp.exp(jax.random.uniform(jax.random.fold_in(own, dim), (parts,), jnp.float32, least / len(cuts), top_value / len(cuts)))
        level = level * jnp.repeat(heights, extent[dim] // parts).reshape([-1 if axis == dim else 1 for axis in range(len(extent))])
    return level


def assign_block(key, own, number, rows, amount, top, reach, skew):
    ranking = jax.random.permutation(key, amount)
    heavy_load, common = shares(amount, rows * top, reach, skew, True), shares(amount, rows * top, reach, skew, False)
    places = jnp.arange(amount)

    def named(tallies, turn):
        used = int((tallies > 0).sum())
        fixed = max(1, used // 4)
        passed = fixed + (places - fixed + turn * (used - fixed)) % max(1, amount - fixed)
        return jnp.zeros((amount,), jnp.int32).at[ranking[jnp.where(places < fixed, places, passed)]].set(jnp.asarray(tallies, jnp.int32))

    tallies = jnp.where(number % 4 == 0, named(heavy_load, number // 4), named(common, number - number // 4 - 1))
    mixed = jax.random.permutation(jax.random.fold_in(own, 3), amount)
    source_of, taker = mixed[0:amount // 2 * 2:2], mixed[1:amount // 2 * 2:2]
    margin = jnp.minimum(tallies[source_of] - 1, reach - tallies[taker]) // 2
    margin = jnp.where((source_of == ranking[0]) | (taker == ranking[0]) | (tallies[taker] == 0), 0, jnp.maximum(margin, 0))
    passed = jax.random.randint(jax.random.fold_in(own, 4), (amount // 2,), 0, 1 << 20) % (margin + 1)
    tallies = tallies.at[source_of].add(-passed).at[taker].add(passed)
    members = jnp.searchsorted(jnp.cumsum(tallies), jnp.arange(rows * top), side="right").astype(jnp.int32)
    table = members.reshape(top, rows).T
    table = table[jax.random.permutation(jax.random.fold_in(own, 1), rows)]
    turn = jax.random.randint(jax.random.fold_in(own, 2), (rows, 1), 0, top)
    return jnp.take_along_axis(table, (jnp.arange(top)[None, :] + turn) % top, axis=1)


def shares(count, total, most, lean, full):
    portions = [(1 << 20) // math.isqrt(grade ** lean) + 1 for grade in range(1, count + 1)]
    largest = most if full else min(most, max(-(-total // count), total * portions[0] // sum(portions)))
    least = 1 if total - largest >= count - 1 else 0
    counts, spare = [largest] + [least] * (count - 1), total - largest - least * (count - 1)
    while spare > 0:
        free = [i for i in range(1, count) if counts[i] < largest] or [i for i in range(1, count) if counts[i] < most]
        mass, budget = sum([portions[i] for i in free]), spare
        for i in free:
            more = min(most - counts[i], max(1, budget * portions[i] // mass), spare)
            counts[i] = counts[i] + more
            spare = spare - more
    return np.array(counts)


def scatter_about(key, dims, scale, most, cuts=(), kind=jnp.bfloat16):
    level = block_levels(key, dims, cuts, -0.22, 0.18) if cuts else 1.0
    drawn = jax.random.normal(key, dims, jnp.float32) * scale * level
    return jnp.minimum(jnp.maximum(drawn, -most), most).astype(kind)


def noise_with(rng, extent, scale, most, shards, heavy, held_as=jnp.bfloat16):
    values = scale * jax.random.normal(rng, extent, jnp.float32)
    if shards:
        values = values * block_levels(rng, extent, shards, -0.22, 0.18)
    return jnp.clip(strengthened(values, jax.random.fold_in(rng, 3), *heavy), -most, most).astype(held_as)


def setup_inputs(seed: int = 0) -> dict:
    splits = jax.random.split(jax.random.key(seed), 12)
    tokens = noise_with(splits[0], (TOKENS, D), 1.0, 24.0, ((0, 128),), (0, 1, 128, 5.5))
    w_in = scatter_about(splits[1], (D, FF), D ** -0.5, 0.21875)
    bias_in = scatter_about(splits[2], (FF,), 0.5, 3.0, (), jnp.float32)
    w_out = scatter_about(splits[3], (FF, D), FF ** -0.5, 0.109375)
    bias_out = scatter_about(splits[4], (D,), 0.5, 3.0, (), jnp.float32)
    gain = jnp.clip(jax.random.uniform(splits[5], (D,), jnp.float32, 0.5, 1.5), 0.5, 1.5)
    shift = scatter_about(splits[6], (D,), 0.1, 0.5, (), jnp.float32)
    slab = draw_slab(jax.random.fold_in(splits[11], 71), 0)
    owners_keys = jax.random.split(jax.random.fold_in(splits[8], 1), QUESTIONS * TOPK // (Q_DEV * TOPK))
    owners_turns = jax.random.permutation(jax.random.fold_in(splits[8], 3), QUESTIONS * TOPK // (Q_DEV * TOPK))
    owners = jax.vmap(lambda own, number: assign_block(jax.random.fold_in(splits[8], 2), own, number, Q_DEV * TOPK, N_INDEX, 1, CAP, 2))(owners_keys, owners_turns).reshape((QUESTIONS, TOPK, 1))
    offsets = set_ends(jax.random.randint(splits[9], (QUESTIONS, TOPK), 0, P_DEV), jax.random.fold_in(splits[9], 1), 0, P_DEV - 1).astype(jnp.int32)
    reader_weights = jnp.clip(jnp.exp(math.log(1.0) - 4.6051702 * jax.random.uniform(splits[10], (QUESTIONS, TOPK), jnp.float32) ** block_levels(splits[10], (QUESTIONS, TOPK), ((0, 128),), -0.2, 0.2)), 0.01, 1.0)
    return dict(tokens=tokens, w_in=w_in, bias_in=bias_in, w_out=w_out, bias_out=bias_out, gain=gain, shift=shift, slab=slab, owners=owners, offsets=offsets, reader_weights=reader_weights)


loss_scale = 256.0
norm_eps = 1e-12

def gelu_tanh(value):
    return jax.nn.gelu(value, approximate=True)

def forward_block(tokens, w_in, bias_in, w_out, bias_out):
    pre = jnp.dot(tokens, w_in, preferred_element_type=jnp.float32) + bias_in
    hidden = gelu_tanh(pre).astype(jnp.bfloat16)
    resid = tokens.astype(jnp.float32) + jnp.dot(hidden, w_out, preferred_element_type=jnp.float32) + bias_out
    centre = lax.optimization_barrier(jnp.mean(resid, axis=-1, keepdims=True))
    spread = lax.optimization_barrier(jnp.mean(jnp.square(resid - centre), axis=-1, keepdims=True))
    rstd = lax.rsqrt(spread + norm_eps)
    normed = (resid - centre) * rstd
    return (pre, hidden, normed, rstd)

def backward_block(tokens, w_in, w_out, gain, pre, normed, rstd, query_grad, length):
    upper = jnp.repeat(query_grad / length, length, axis=0) * gain
    resid_grad = (upper - lax.optimization_barrier(jnp.mean(upper, axis=-1, keepdims=True)) - normed * lax.optimization_barrier(jnp.mean(upper * normed, axis=-1, keepdims=True))) * rstd
    out_grad = resid_grad.astype(jnp.bfloat16)
    hid_grad = jnp.dot(out_grad, w_out.T, preferred_element_type=jnp.float32)
    _, pull = jax.vjp(gelu_tanh, pre)
    pre_grad = pull(hid_grad)[0].astype(jnp.bfloat16)
    token_grads = (resid_grad + jnp.dot(pre_grad, w_in.T, preferred_element_type=jnp.float32)).astype(jnp.bfloat16)
    return (out_grad, pre_grad, token_grads)

def reference(tokens, w_in, bias_in, w_out, bias_out, gain, shift, slab, owners, offsets, reader_weights):
    blocks = N_QUERY * N_INDEX
    tok_blocks = tokens.reshape(blocks, Q_DEV * LEN, D)
    own_blocks = owners.reshape(blocks, Q_DEV, TOPK)
    off_blocks = offsets.reshape(blocks, Q_DEV, TOPK)
    read_blocks = reader_weights.reshape(blocks, Q_DEV, TOPK)

    def step(total, pieces):
        block_tok, block_own, block_off, block_read = pieces
        pre, hidden, normed, rstd = forward_block(block_tok, w_in, bias_in, w_out, bias_out)
        query = lax.optimization_barrier(jnp.mean((normed * gain + shift).reshape(Q_DEV, LEN, D), axis=1))
        where = (block_own * P_DEV + block_off).astype(jnp.int32)
        rows = slab[where]
        scores = jnp.einsum('qd,qkd->qk', query, rows.astype(jnp.float32), precision=lax.Precision.HIGHEST)
        prob = jax.nn.softmax(scores, axis=-1)
        target = block_read / lax.optimization_barrier(jnp.sum(block_read, axis=-1, keepdims=True))
        coef = loss_scale * (prob - target)
        query_grad = jnp.einsum('qk,qkd->qd', coef, rows.astype(jnp.float32), precision=lax.Precision.HIGHEST)
        out_grad, pre_grad, token_grads = backward_block(block_tok, w_in, w_out, gain, pre, normed, rstd, query_grad, LEN)
        term = jnp.concatenate([jnp.dot(pre_grad.T, block_tok, preferred_element_type=jnp.float32), jnp.dot(hidden.T, out_grad, preferred_element_type=jnp.float32)], axis=1)
        return (total + term, token_grads)
    start = jnp.zeros((FF, 2 * D), jnp.float32)
    total, grads = lax.scan(step, start, (tok_blocks, own_blocks, off_blocks, read_blocks))
    return (grads.reshape(blocks * Q_DEV * LEN, D), total / (N_QUERY * N_INDEX))
```

```python
import jax
import jax.numpy as jnp
from jax import lax
from jax.sharding import PartitionSpec as P

loss_scale = 256.0
norm_eps = 1e-12
every = ("query", "index")


def shifted(value, core, along_y):
    pairs = []
    for query in range(8):
        y, c = query // 2, query % 2
        to = ((y + along_y) % 4) * 2 + (c + core) % 2
        pairs += [(query * 16 + i, to * 16 + i) for i in range(16)]
    return lax.ppermute(value, every, pairs)


def pair_sum(part):
    cols = part.shape[1]
    core = lax.axis_index("query") % 2
    whole = part.reshape(4, 2, 16, 24, cols)
    away = lax.dynamic_index_in_dim(whole, 1 - core, 1, keepdims=False).astype(jnp.bfloat16)
    kept = lax.dynamic_index_in_dim(whole, core, 1, keepdims=False)
    return kept + shifted(away, 1, 0).astype(jnp.float32)


def over_y(value):
    y = lax.axis_index("query") // 2
    total = lax.dynamic_index_in_dim(value, y, 0, keepdims=False)
    got = []
    for step in (1, 3, 2):
        away = lax.dynamic_index_in_dim(value, (y + step) % 4, 0, keepdims=False)
        got.append(shifted(away.astype(jnp.bfloat16), 0, step))
    for piece in got:
        total = total + piece.astype(jnp.float32)
    return total


def over_index(value):
    came = lax.all_to_all(value.astype(jnp.bfloat16), "index", 0, 0, tiled=True)
    return jnp.sum(came.astype(jnp.float32), axis=0)


def summed_rows(part):
    chip = pair_sum(part)
    half = chip.shape[-1] // 2
    left = over_index(over_y(chip[..., :half]))
    right = over_y(over_index(chip[..., half:].transpose(1, 0, 2, 3)))
    return jnp.concatenate([left, right], axis=1)


def gelu_tanh(value):
    return jax.nn.gelu(value, approximate=True)


def body(
    tokens, w_in, bias_in, w_out, bias_out, gain, shift, slab, owners, offsets, reader_weights
):
    shards = lax.axis_size("index")
    devices = lax.axis_size("query") * lax.axis_size("index")
    questions = offsets.shape[0]
    picks = offsets.shape[1]
    width = tokens.shape[1]
    length = tokens.shape[0] // questions
    slots = questions * picks
    capacity = 3 * slots // shards
    flat_owner = owners.reshape(slots)
    flat_offset = offsets.reshape(slots)
    member = (flat_owner[:, None] == jnp.arange(shards, dtype=jnp.int32)[None, :]).astype(jnp.int32)
    before = jnp.cumsum(member, axis=0) - member
    rank_in = jnp.sum(before * member, axis=1)
    position = flat_owner * capacity + rank_in
    pre = jnp.dot(tokens, w_in, preferred_element_type=jnp.float32) + bias_in
    hidden = gelu_tanh(pre).astype(jnp.bfloat16)
    resid = (
        tokens.astype(jnp.float32)
        + jnp.dot(hidden, w_out, preferred_element_type=jnp.float32)
        + bias_out
    )
    centre = jnp.mean(resid, axis=-1, keepdims=True)
    spread = jnp.mean(jnp.square(resid - centre), axis=-1, keepdims=True)
    rstd = lax.rsqrt(spread + norm_eps)
    normed = (resid - centre) * rstd
    query = jnp.mean((normed * gain + shift).reshape(questions, length, width), axis=1)
    target = reader_weights / jnp.sum(reader_weights, axis=-1, keepdims=True)
    wanted = jnp.zeros((shards * capacity,), jnp.int32).at[position].set(flat_offset)
    arrived = lax.all_to_all(
        wanted.reshape(shards, capacity), "index", split_axis=0, concat_axis=0, tiled=True
    )
    fetched = slab[arrived.reshape(shards * capacity)].reshape(shards, capacity, width)
    returned = lax.all_to_all(fetched, "index", split_axis=0, concat_axis=0, tiled=True)
    rows = returned.reshape(shards * capacity, width)[position].reshape(questions, picks, width)
    rows_wide = rows.astype(jnp.float32)
    scores = jnp.einsum("qd,qkd->qk", query, rows_wide, precision=lax.Precision.HIGHEST)
    prob = jax.nn.softmax(scores, axis=-1)
    coef = loss_scale * (prob - target)
    query_grad = jnp.einsum("qk,qkd->qd", coef, rows_wide, precision=lax.Precision.HIGHEST)
    upper = jnp.repeat(query_grad / length, length, axis=0) * gain
    resid_grad = (
        upper
        - jnp.mean(upper, axis=-1, keepdims=True)
        - normed * jnp.mean(upper * normed, axis=-1, keepdims=True)
    ) * rstd
    out_grad = resid_grad.astype(jnp.bfloat16)
    hid_grad = jnp.dot(out_grad, w_out.T, preferred_element_type=jnp.float32)
    _, pull = jax.vjp(gelu_tanh, pre)
    pre_grad = pull(hid_grad)[0].astype(jnp.bfloat16)
    token_grads = (
        resid_grad + jnp.dot(pre_grad, w_in.T, preferred_element_type=jnp.float32)
    ).astype(jnp.bfloat16)
    first = lax.dot_general(
        pre_grad, tokens, (((0,), (0,)), ((), ())), preferred_element_type=jnp.float32
    )
    second = lax.dot_general(
        hidden, out_grad, (((0,), (0,)), ((), ())), preferred_element_type=jnp.float32
    )
    summed = jnp.concatenate([summed_rows(first), summed_rows(second)], axis=1)
    return (token_grads, summed / devices)


def solution(mesh):
    placed = (
        P(("query", "index"), None),
        P(),
        P(),
        P(),
        P(),
        P(),
        P(),
        P("index", None),
        P(("query", "index"), None, None),
        P(("query", "index"), None),
        P(("query", "index"), None),
    )
    return jax.shard_map(
        body,
        mesh=mesh,
        in_specs=placed,
        out_specs=(P(("query", "index"), None), P(("query", "index"), None)),
        check_vma=False,
    )
```

```python
import jax
import jax.numpy as jnp
from jax import lax
from jax.experimental import pallas as pl
from jax.experimental.pallas import tpu as pltpu
from jax.sharding import PartitionSpec as P

loss_scale = 256.0
norm_eps = 1e-12
every = ("query", "index")
MIB = 1 << 20
low = -1e30
params = pltpu.CompilerParams(vmem_limit_bytes=56 * MIB)
light = pl.CostEstimate(flops=1000, bytes_accessed=1000, transcendentals=0)
anywhere = pl.BlockSpec(memory_space=pl.ANY)


def halves(value):
    first = value.astype(jnp.bfloat16)
    return first, (value - first.astype(jnp.float32)).astype(jnp.bfloat16)


def dot_rows(left, right):
    return lax.dot_general(left, right, (((1,), (1,)), ((), ())), preferred_element_type=jnp.float32)


def columns_dot(left, right):
    return lax.dot_general(left, right, (((0,), (0,)), ((), ())), preferred_element_type=jnp.float32)


def exchange(value):
    return lax.all_to_all(value, "index", 0, 0, tiled=True)


def shifted(value, core, along_y):
    pairs = []
    for query in range(8):
        y, c = query // 2, query % 2
        to = ((y + along_y) % 4) * 2 + (c + core) % 2
        pairs += [(query * 16 + i, to * 16 + i) for i in range(16)]
    return lax.ppermute(value, every, pairs)


def whole(*shape):
    return pl.BlockSpec(shape, lambda *_: (0,) * len(shape))


def slope(pre):
    square = pre * pre
    bend = jnp.tanh(pre * (0.7978845608028654 + 0.035677408136300125 * square))
    share = 0.5 + 0.5 * bend
    value = pre * share
    grad = share + (value - value * share) * (1.5957691216057308 + 0.21406444881780074 * square)
    return value, grad


def forward_kernel(
    tokens_ref, w_in_ref, bias_in_ref, w_out_ref, bias_out_ref, gain_ref, shift_ref, table_ref,
    hidden_ref, slope_ref, normed_ref, rstd_ref, ask_ref, resid, query,
):
    step = pl.program_id(0)

    @pl.when(step == 0)
    def _():
        resid[...] = tokens_ref[...].astype(jnp.float32) + bias_out_ref[...]

    for part in range(4):
        rows = slice(part * 256, part * 256 + 256)
        pre = jnp.dot(tokens_ref[rows, :], w_in_ref[...], preferred_element_type=jnp.float32) + bias_in_ref[...]
        value, grad = slope(pre)
        value = value.astype(jnp.bfloat16)
        hidden_ref[rows, :] = value
        slope_ref[rows, :] = grad.astype(jnp.bfloat16)
        resid[rows, :] += jnp.dot(value, w_out_ref[...], preferred_element_type=jnp.float32)

    @pl.when(step == pl.num_programs(0) - 1)
    def _():
        for q in range(16):
            rows = slice(q * 64, q * 64 + 64)
            here = resid[rows, :]
            away = here - jnp.mean(here, axis=-1, keepdims=True)
            rstd = lax.rsqrt(jnp.mean(away * away, axis=-1, keepdims=True) + norm_eps)
            normed = away * rstd
            normed_ref[rows, :] = normed
            rstd_ref[rows, :] = rstd
            query[q : q + 1, :] = (
                jnp.sum(normed, axis=0, keepdims=True) * (1 / 64) * gain_ref[...] + shift_ref[...]
            )
        upper, lower = halves(query[...])
        for to in range(16):
            ask_ref[to, :, :768] = upper
            ask_ref[to, :, 768:1536] = lower
            ask_ref[to, :, 1536:] = table_ref[...]


def forward(tokens, w_in, bias_in, w_out, bias_out, gain, shift, table):
    block = 512
    units = pl.BlockSpec((1024, block), lambda j: (0, j))
    return pl.pallas_call(
        forward_kernel,
        grid=(3072 // block,),
        in_specs=[
            whole(1024, 768),
            pl.BlockSpec((768, block), lambda j: (0, j)),
            pl.BlockSpec((1, block), lambda j: (0, j)),
            pl.BlockSpec((block, 768), lambda j: (j, 0)),
            whole(1, 768),
            whole(1, 768),
            whole(1, 768),
            whole(16, 512),
        ],
        out_specs=(units, units, whole(1024, 768), whole(1024, 1), whole(16, 16, 2048)),
        out_shape=(
            jax.ShapeDtypeStruct((1024, 3072), jnp.bfloat16),
            jax.ShapeDtypeStruct((1024, 3072), jnp.bfloat16),
            jax.ShapeDtypeStruct((1024, 768), jnp.float32),
            jax.ShapeDtypeStruct((1024, 1), jnp.float32),
            jax.ShapeDtypeStruct((16, 16, 2048), jnp.bfloat16),
        ),
        scratch_shapes=[pltpu.VMEM((1024, 768), jnp.float32), pltpu.VMEM((16, 768), jnp.float32)],
        compiler_params=params,
        cost_estimate=light,
    )(
        tokens, w_in, bias_in.reshape(1, -1), w_out, bias_out.reshape(1, -1),
        gain.reshape(1, -1), shift.reshape(1, -1), table,
    )


def score_kernel(
    me_ref, ask_ref, slab_hbm, weight_ref, share_ref, stat_ref, count, scores, slab, sems
):
    loads = []
    for block in range(8):
        rows = pl.ds(block * 512, 512)
        loads.append(pltpu.make_async_copy(slab_hbm.at[rows], slab.at[rows], sems.at[block]))
        loads[-1].start()
    me = me_ref[0].astype(jnp.float32)
    turn = (lax.broadcasted_iota(jnp.int32, (1, 512), 1) // 64).astype(jnp.float32)
    row = lax.broadcasted_iota(jnp.int32, (256, 512), 0).astype(jnp.float32)
    line = lax.broadcasted_iota(jnp.int32, (128, 512), 0).astype(jnp.float32)

    def source(s, carry):
        meta = ask_ref[s, :, 1536:].astype(jnp.float32)
        for g in range(2):
            owner, high, spot, upper, lower = [meta[2 * f + g : 2 * f + g + 1] for f in range(5)]
            key = jnp.where(owner == me, high * 8.0 + turn, -1.0)
            left = jnp.where(row == key, 1.0, 0.0).astype(jnp.bfloat16)
            hit = line == spot
            right = jnp.concatenate(
                [jnp.where(hit, 1.0, 0.0), jnp.where(hit, upper, 0.0), jnp.where(hit, lower, 0.0)], axis=0
            ).astype(jnp.bfloat16)
            out = dot_rows(left, right)
            at = pl.ds(pl.multiple_of(s * 16 + g * 8, 8), 8)
            count[:, at, :] = out[:, :128].reshape(32, 8, 128)
            share_ref[:, at, :] = (out[:, 128:256] + out[:, 256:]).reshape(32, 8, 128)
        return carry

    lax.fori_loop(0, 16, source, 0, unroll=2)
    both = jnp.concatenate(
        [ask_ref[:, :, :768].reshape(256, 768), ask_ref[:, :, 768:1536].reshape(256, 768)], axis=0
    )
    top = jnp.full((256, 128), low, jnp.float32)
    for block in range(8):
        loads[block].wait()
        got = dot_rows(both, slab[block * 512 : block * 512 + 512])
        got = got[:256] + got[256:]
        for i in range(4):
            part = got[:, i * 128 : i * 128 + 128]
            scores[block * 4 + i] = part
            top = jnp.maximum(top, jnp.where(count[block * 4 + i] > 0, part, low))
    top = jnp.max(top, axis=1, keepdims=True)
    mass = jnp.zeros((256, 128), jnp.float32)
    for high in range(32):
        here = count[high]
        part = jnp.where(here > 0, here * jnp.exp(jnp.minimum(scores[high] - top, 0.0)), 0.0)
        mass = mass + part
        weight_ref[high] = part
    mass = jnp.sum(mass, axis=1, keepdims=True)
    lane = lax.broadcasted_iota(jnp.int32, (256, 128), 1)
    stat = jnp.transpose(jnp.where(lane == 0, top, mass))[:8]
    for to in range(16):
        stat_ref[to] = stat


def score(me, asked, slab):
    vmem = pl.BlockSpec(memory_space=pltpu.VMEM)
    return pl.pallas_call(
        score_kernel,
        out_shape=(
            jax.ShapeDtypeStruct((32, 256, 128), jnp.float32),
            jax.ShapeDtypeStruct((32, 256, 128), jnp.float32),
            jax.ShapeDtypeStruct((16, 8, 256), jnp.float32),
        ),
        in_specs=[pl.BlockSpec(memory_space=pltpu.SMEM), vmem, anywhere],
        out_specs=(vmem, vmem, vmem),
        scratch_shapes=[
            pltpu.VMEM((32, 256, 128), jnp.float32),
            pltpu.VMEM((32, 256, 128), jnp.float32),
            pltpu.VMEM((4096, 768), jnp.bfloat16),
            pltpu.SemaphoreType.DMA((8,)),
        ],
        compiler_params=params,
        cost_estimate=light,
    )(me, asked, slab)


def pull_kernel(me_ref, stat_ref, weight_ref, share_ref, slab_ref, out_ref, factor, total):
    step = pl.program_id(0)

    @pl.when(step == 0)
    def _():
        stats = stat_ref[...]
        tops, masses = stats[:, 0], stats[:, 1]
        best = jnp.max(tops, axis=0, keepdims=True)
        mass = jnp.sum(jnp.exp(tops - best) * masses, axis=0, keepdims=True)
        mine = stat_ref[me_ref[0]][0:1]
        line = loss_scale * jnp.exp(mine - best) / mass
        factor[...] = jnp.transpose(jnp.broadcast_to(line, (128, 256)))
        total[...] = jnp.zeros_like(total)

    coef = jnp.concatenate(
        [weight_ref[i] * factor[...] - loss_scale * share_ref[i] for i in range(4)], axis=1
    )
    both = jnp.concatenate(halves(coef), axis=0)
    got = jnp.dot(both, slab_ref[...], preferred_element_type=jnp.float32)
    total[...] += got[:256] + got[256:]

    @pl.when(step == 7)
    def _():
        out_ref[...] = total[...].astype(jnp.bfloat16)


def pull(me, stats, weight, share, slab):
    quarter = pl.BlockSpec((4, 256, 128), lambda j, me: (j, 0, 0))
    return pl.pallas_call(
        pull_kernel,
        grid_spec=pltpu.PrefetchScalarGridSpec(
            num_scalar_prefetch=1,
            grid=(8,),
            in_specs=[whole(16, 8, 256), quarter, quarter, pl.BlockSpec((512, 768), lambda j, me: (j, 0))],
            out_specs=whole(256, 768),
            scratch_shapes=[pltpu.VMEM((256, 128), jnp.float32), pltpu.VMEM((256, 768), jnp.float32)],
        ),
        out_shape=jax.ShapeDtypeStruct((256, 768), jnp.bfloat16),
        compiler_params=params,
        cost_estimate=light,
    )(me, stats, weight, share, slab)


def resid_kernel(came_ref, normed_ref, rstd_ref, gain_ref, resid_grad_ref, out_grad_ref, ups):
    step = pl.program_id(0)

    @pl.when(step == 0)
    def _():
        ups[...] = jnp.sum(came_ref[...].astype(jnp.float32), axis=0) * (1 / 64) * gain_ref[...]

    for q in range(4):
        up = ups[pl.ds(step * 4 + q, 1), :]
        rows = slice(q * 64, q * 64 + 64)
        normed = normed_ref[rows, :]
        along = jnp.mean(up * normed, axis=-1, keepdims=True)
        grad = (up - jnp.mean(up, axis=-1, keepdims=True) - normed * along) * rstd_ref[rows, :]
        resid_grad_ref[rows, :] = grad
        out_grad_ref[rows, :] = grad.astype(jnp.bfloat16)


def resid_gradient(came, normed, rstd, gain):
    rows = pl.BlockSpec((256, 768), lambda j: (j, 0))
    return pl.pallas_call(
        resid_kernel,
        grid=(4,),
        in_specs=[
            whole(16, 16, 768),
            rows,
            pl.BlockSpec((256, 1), lambda j: (j, 0)),
            whole(1, 768),
        ],
        out_specs=(rows, rows),
        out_shape=(
            jax.ShapeDtypeStruct((1024, 768), jnp.float32),
            jax.ShapeDtypeStruct((1024, 768), jnp.bfloat16),
        ),
        scratch_shapes=[pltpu.VMEM((16, 768), jnp.float32)],
        compiler_params=params,
        cost_estimate=light,
    )(came, normed, rstd, gain.reshape(1, -1))


def pair_kernel(place_ref, grad_ref, came_ref, *refs):
    own_ref, one_ref, three_ref, two_ref, right_ref = refs[-5:]
    for out, step in ((own_ref, 0), (one_ref, 1), (three_ref, 3), (two_ref, 2)):
        at = (place_ref[1] + step) % 4
        got = grad_ref[at, 0, :, :384] + came_ref[at, :, :384].astype(jnp.float32)
        out[...] = got.astype(out.dtype)
    right = [grad_ref[y, 0, :, 384:] + came_ref[y, :, 384:].astype(jnp.float32) for y in range(4)]
    for i in range(2):
        rows = slice(i * 24, i * 24 + 24)
        right_ref[i] = jnp.concatenate([part[rows] for part in right], axis=0).astype(jnp.bfloat16)


def pair(place, grad, came, *after):
    piece = pl.BlockSpec((48, 384), lambda j, place: (j, 0))
    return pl.pallas_call(
        pair_kernel,
        grid_spec=pltpu.PrefetchScalarGridSpec(
            num_scalar_prefetch=1,
            grid=(8,),
            in_specs=[
                pl.BlockSpec((4, 1, 48, 768), lambda j, place: (0, place[0], j, 0)),
                pl.BlockSpec((4, 48, 768), lambda j, place: (0, j, 0)),
            ]
            + [anywhere] * len(after),
            out_specs=(piece,) * 4 + (pl.BlockSpec((2, 96, 384), lambda j, place: (j, 0, 0)),),
        ),
        out_shape=(jax.ShapeDtypeStruct((384, 384), jnp.float32),)
        + (jax.ShapeDtypeStruct((384, 384), jnp.bfloat16),) * 3
        + (jax.ShapeDtypeStruct((16, 96, 384), jnp.bfloat16),),
        compiler_params=params,
        cost_estimate=light,
    )(place, grad, came, *after)


def away_part(grad, core):
    return lax.dynamic_index_in_dim(grad, 1 - core, 1, keepdims=False).astype(jnp.bfloat16)


def left_kernel(own_a, one_a, three_a, two_a, own_b, one_b, three_b, two_b, *refs):
    out_ref = refs[-1]
    for side, own, parts in ((0, own_a, (one_a, three_a, two_a)), (1, own_b, (one_b, three_b, two_b))):
        total = own[...]
        for part in parts:
            total = total + part[...].astype(jnp.float32)
        out_ref[:, side * 384 : side * 384 + 384] = total.astype(jnp.bfloat16)


def left_sums(first, second, *after):
    vmem = pl.BlockSpec(memory_space=pltpu.VMEM)
    return pl.pallas_call(
        left_kernel,
        in_specs=[vmem] * 8 + [anywhere] * len(after),
        out_specs=vmem,
        out_shape=jax.ShapeDtypeStruct((384, 768), jnp.bfloat16),
        compiler_params=params,
        cost_estimate=light,
    )(*first, *second, *after)


def right_kernel(y_ref, first_ref, second_ref, own_ref, one_ref, three_ref, two_ref, total):
    total[:, :384] = jnp.sum(first_ref[...].astype(jnp.float32), axis=0)
    total[:, 384:] = jnp.sum(second_ref[...].astype(jnp.float32), axis=0)
    for out, step in ((own_ref, 0), (one_ref, 1), (three_ref, 3), (two_ref, 2)):
        at = (y_ref[0] + step) % 4
        out[...] = total[pl.ds(pl.multiple_of(at * 24, 8), 24), :]


def right_sums(y, first, second):
    vmem = pl.BlockSpec(memory_space=pltpu.VMEM)
    return pl.pallas_call(
        right_kernel,
        in_specs=[pl.BlockSpec(memory_space=pltpu.SMEM), vmem, vmem],
        out_specs=(vmem,) * 4,
        out_shape=(jax.ShapeDtypeStruct((24, 768), jnp.float32),) * 4,
        scratch_shapes=[pltpu.VMEM((96, 768), jnp.float32)],
        compiler_params=params,
        cost_estimate=light,
    )(y, first, second)


def last_kernel(devices, left_ref, own_ref, one_ref, three_ref, two_ref, out_ref):
    left = jnp.sum(left_ref[...].astype(jnp.float32), axis=0) / devices
    right = (own_ref[...] + one_ref[...] + three_ref[...] + two_ref[...]) / devices
    for side in range(2):
        cols = slice(side * 384, side * 384 + 384)
        out_ref[:, side * 768 : side * 768 + 384] = left[:, cols]
        out_ref[:, side * 768 + 384 : side * 768 + 768] = right[:, cols]


def last_sums(devices, left, *right):
    vmem = pl.BlockSpec(memory_space=pltpu.VMEM)
    return pl.pallas_call(
        lambda *refs: last_kernel(devices, *refs),
        in_specs=[vmem] * 5,
        out_specs=vmem,
        out_shape=jax.ShapeDtypeStruct((24, 1536), jnp.float32),
        compiler_params=params,
        cost_estimate=light,
    )(left, *right)


def body(
    tokens, w_in, bias_in, w_out, bias_out, gain, shift, slab, owners, offsets, reader_weights
):
    devices = lax.axis_size("query") * lax.axis_size("index")
    me = lax.axis_index("index")[None]
    y = lax.axis_index("query") // 2
    core = lax.axis_index("query") % 2
    place = jnp.stack([core, y])

    target = reader_weights / jnp.sum(reader_weights, axis=-1, keepdims=True)
    fields = (owners[..., 0], offsets // 128, offsets % 128) + halves(target)
    table = jnp.stack([field.astype(jnp.bfloat16).reshape(2, 512) for field in fields]).reshape(10, 512)
    table = jnp.pad(table, ((0, 6), (0, 0)))

    hidden, slopes, normed, rstd, ask = forward(
        tokens, w_in, bias_in, w_out, bias_out, gain, shift, table
    )
    weight, share, stat = score(me, exchange(ask), slab)
    partial = pull(me, exchange(stat), weight, share, slab)
    came = exchange(partial.reshape(16, 16, 768))
    resid_grad, out_grad = resid_gradient(came, normed, rstd, gain)

    def stage_one(left, right, *after):
        grad = columns_dot(left, right).reshape(4, 2, 384, 768)
        over_core = shifted(away_part(grad, core), 1, 0)
        own, one, three, two, packed = pair(place, grad, over_core, *after)
        moved = [shifted(piece, 0, step) for piece, step in ((one, 1), (three, 3), (two, 2))]
        return (own, *moved), exchange(packed)

    left_second, right_second = stage_one(hidden, out_grad)
    pre_grad = (
        jnp.dot(out_grad, w_out.T, preferred_element_type=jnp.float32) * slopes.astype(jnp.float32)
    ).astype(jnp.bfloat16)
    left_first, right_first = stage_one(pre_grad, tokens, right_second)
    token_grads = (
        resid_grad + jnp.dot(pre_grad, w_in.T, preferred_element_type=jnp.float32)
    ).astype(jnp.bfloat16)

    left = exchange(left_sums(left_first, left_second, token_grads).reshape(16, 24, 768))
    own, one, three, two = right_sums(y[None], right_first, right_second)
    right = [own] + [shifted(piece, 0, step) for piece, step in ((one, 1), (three, 3), (two, 2))]
    return (token_grads, last_sums(devices, left, *right))


def solution(mesh):
    placed = (
        P(("query", "index"), None),
        P(),
        P(),
        P(),
        P(),
        P(),
        P(),
        P("index", None),
        P(("query", "index"), None, None),
        P(("query", "index"), None),
        P(("query", "index"), None),
    )
    return jax.shard_map(
        body,
        mesh=mesh,
        in_specs=placed,
        out_specs=(P(("query", "index"), None), P(("query", "index"), None)),
        check_vma=False,
    )
```

```python
import jax
import jax.numpy as jnp
from jax import lax
from jax.experimental import pallas as pl
from jax.experimental.pallas import tpu as pltpu
from jax.sharding import PartitionSpec as P

loss_scale = 256.0
norm_eps = 1e-12
every = ("query", "index")
MIB = 1 << 20
low = -1e30


def limit(mib):
    return pltpu.CompilerParams(vmem_limit_bytes=mib * MIB)


def cost(us):
    return pl.CostEstimate(flops=us * 1_000_000_000, bytes_accessed=1000, transcendentals=0)
anywhere = pl.BlockSpec(memory_space=pl.ANY)


def halves(value):
    first = value.astype(jnp.bfloat16)
    return first, (value - first.astype(jnp.float32)).astype(jnp.bfloat16)


def dot_rows(left, right):
    return lax.dot_general(left, right, (((1,), (1,)), ((), ())), preferred_element_type=jnp.float32)


def columns_dot(left, right):
    return lax.dot_general(left, right, (((0,), (0,)), ((), ())), preferred_element_type=jnp.float32)


def exchange(value):
    return lax.all_to_all(value, "index", 0, 0, tiled=True)


def shifted(value, core, along_y):
    pairs = []
    for query in range(8):
        y, c = query // 2, query % 2
        to = ((y + along_y) % 4) * 2 + (c + core) % 2
        pairs += [(query * 16 + i, to * 16 + i) for i in range(16)]
    return lax.ppermute(value, every, pairs)


def whole(*shape):
    return pl.BlockSpec(shape, lambda *_: (0,) * len(shape))


def slope(pre):
    square = pre * pre
    bend = jnp.tanh(pre * (0.7978845608028654 + 0.035677408136300125 * square))
    share = 0.5 + 0.5 * bend
    value = pre * share
    grad = share + (value - value * share) * (1.5957691216057308 + 0.21406444881780074 * square)
    return value, grad


def forward_kernel(
    tokens_ref, w_in_ref, bias_in_ref, w_out_ref, vectors_ref,
    hidden_ref, slope_ref, normed_ref, rstd_ref, ask_ref, resid, query,
):
    step = pl.program_id(0)

    @pl.when(step == 0)
    def _():
        resid[...] = tokens_ref[...].astype(jnp.float32) + vectors_ref[:, :768]

    for part in range(4):
        rows = slice(part * 256, part * 256 + 256)
        pre = jnp.dot(tokens_ref[rows, :], w_in_ref[...], preferred_element_type=jnp.float32) + bias_in_ref[...]
        value, grad = slope(pre)
        value = value.astype(jnp.bfloat16)
        hidden_ref[rows, :] = value
        slope_ref[rows, :] = grad.astype(jnp.bfloat16)
        resid[rows, :] += jnp.dot(value, w_out_ref[...], preferred_element_type=jnp.float32)

    @pl.when(step == pl.num_programs(0) - 1)
    def _():
        for q in range(16):
            rows = slice(q * 64, q * 64 + 64)
            here = resid[rows, :]
            away = here - jnp.mean(here, axis=-1, keepdims=True)
            rstd = lax.rsqrt(jnp.mean(away * away, axis=-1, keepdims=True) + norm_eps)
            normed = away * rstd
            normed_ref[rows, :] = normed
            rstd_ref[rows, :] = rstd
            query[q : q + 1, :] = (
                jnp.sum(normed, axis=0, keepdims=True) * (1 / 64) * vectors_ref[:, 768:1536] + vectors_ref[:, 1536:2304]
            )
        upper, lower = halves(query[...])
        for to in range(16):
            ask_ref[to, :, :768] = upper
            ask_ref[to, :, 768:] = lower


def forward(tokens, w_in, bias_in, w_out, vectors):
    block = 512
    units = pl.BlockSpec((1024, block), lambda j: (0, j))
    return pl.pallas_call(
        forward_kernel,
        grid=(3072 // block,),
        in_specs=[
            whole(1024, 768),
            pl.BlockSpec((768, block), lambda j: (0, j)),
            pl.BlockSpec((1, block), lambda j: (0, j)),
            pl.BlockSpec((block, 768), lambda j: (j, 0)),
            whole(1, 3072),
        ],
        out_specs=(units, units, whole(1024, 768), whole(1024, 1), whole(16, 16, 1536)),
        out_shape=(
            jax.ShapeDtypeStruct((1024, 3072), jnp.bfloat16),
            jax.ShapeDtypeStruct((1024, 3072), jnp.bfloat16),
            jax.ShapeDtypeStruct((1024, 768), jnp.float32),
            jax.ShapeDtypeStruct((1024, 1), jnp.float32),
            jax.ShapeDtypeStruct((16, 16, 1536), jnp.bfloat16),
        ),
        scratch_shapes=[pltpu.VMEM((1024, 768), jnp.float32), pltpu.VMEM((16, 768), jnp.float32)],
        compiler_params=limit(36),
        cost_estimate=cost(20),
    )(tokens, w_in, bias_in.reshape(1, -1), w_out, vectors)


def table_kernel(owner_ref, offset_ref, weight_ref, out_ref):
    weight = weight_ref[...]
    target = weight / jnp.sum(weight, axis=-1, keepdims=True)
    offset = offset_ref[...]
    upper, lower = halves(target)
    fields = [
        owner_ref[...].astype(jnp.float32),
        (offset // 128).astype(jnp.float32),
        (offset % 128).astype(jnp.float32),
        upper.astype(jnp.float32),
        lower.astype(jnp.float32),
    ]
    rows = [
        jnp.concatenate([field[g * 8 + i : g * 8 + i + 1] for i in range(8)], axis=1)
        for field in fields
        for g in range(2)
    ]
    rows = jnp.concatenate(rows + [jnp.zeros((6, 512), jnp.float32)], axis=0).astype(jnp.bfloat16)
    for to in range(16):
        out_ref[to] = rows


def table(owners, offsets, reader_weights):
    vmem = pl.BlockSpec(memory_space=pltpu.VMEM)
    return pl.pallas_call(
        table_kernel,
        in_specs=[vmem] * 3,
        out_specs=vmem,
        out_shape=jax.ShapeDtypeStruct((16, 16, 512), jnp.bfloat16),
        compiler_params=limit(16),
        cost_estimate=cost(1),
    )(owners, offsets, reader_weights)


def picks_kernel(me_ref, table_ref, after_ref, count_ref, share_ref):
    me = me_ref[0].astype(jnp.float32)
    turn = (lax.broadcasted_iota(jnp.int32, (1, 512), 1) // 64).astype(jnp.float32)
    row = lax.broadcasted_iota(jnp.int32, (256, 512), 0).astype(jnp.float32)
    line = lax.broadcasted_iota(jnp.int32, (128, 512), 0).astype(jnp.float32)

    def source(s, carry):
        meta = table_ref[s].astype(jnp.float32)
        for g in range(2):
            owner, high, spot, upper, lower = [meta[2 * f + g : 2 * f + g + 1] for f in range(5)]
            key = jnp.where(owner == me, high * 8.0 + turn, -1.0)
            left = jnp.where(row == key, 1.0, 0.0).astype(jnp.bfloat16)
            hit = line == spot
            right = jnp.concatenate(
                [jnp.where(hit, 1.0, 0.0), jnp.where(hit, upper, 0.0), jnp.where(hit, lower, 0.0)], axis=0
            ).astype(jnp.bfloat16)
            out = dot_rows(left, right)
            at = pl.ds(pl.multiple_of(s * 16 + g * 8, 8), 8)
            count_ref[:, at, :] = out[:, :128].reshape(32, 8, 128)
            share_ref[:, at, :] = (out[:, 128:256] + out[:, 256:]).reshape(32, 8, 128)
        return carry

    lax.fori_loop(0, 16, source, 0, unroll=2)


def picks(me, asked, after):
    vmem = pl.BlockSpec(memory_space=pltpu.VMEM)
    return pl.pallas_call(
        picks_kernel,
        out_shape=(jax.ShapeDtypeStruct((32, 256, 128), jnp.float32),) * 2,
        in_specs=[pl.BlockSpec(memory_space=pltpu.SMEM), vmem, anywhere],
        out_specs=(vmem, vmem),
        compiler_params=limit(24),
        cost_estimate=cost(10),
    )(me, asked, after)


def score_kernel(ask_ref, count_ref, slab_hbm, weight_ref, stat_ref, scores, slab, sems):
    loads = []
    for block in range(8):
        rows = pl.ds(block * 512, 512)
        loads.append(pltpu.make_async_copy(slab_hbm.at[rows], slab.at[rows], sems.at[block]))
        loads[-1].start()
    both = jnp.concatenate(
        [ask_ref[:, :, :768].reshape(256, 768), ask_ref[:, :, 768:].reshape(256, 768)], axis=0
    )
    top = jnp.full((256, 128), low, jnp.float32)
    for block in range(8):
        loads[block].wait()
        got = dot_rows(both, slab[block * 512 : block * 512 + 512])
        got = got[:256] + got[256:]
        for i in range(4):
            part = got[:, i * 128 : i * 128 + 128]
            scores[block * 4 + i] = part
            top = jnp.maximum(top, jnp.where(count_ref[block * 4 + i] > 0, part, low))
    top = jnp.max(top, axis=1, keepdims=True)
    mass = jnp.zeros((256, 128), jnp.float32)
    for high in range(32):
        here = count_ref[high]
        part = jnp.where(here > 0, here * jnp.exp(jnp.minimum(scores[high] - top, 0.0)), 0.0)
        mass = mass + part
        weight_ref[high] = part
    mass = jnp.sum(mass, axis=1, keepdims=True)
    lane = lax.broadcasted_iota(jnp.int32, (256, 128), 1)
    stat = jnp.transpose(jnp.where(lane == 0, top, mass))[:8]
    for to in range(16):
        stat_ref[to] = stat


def score(asked, count, slab):
    vmem = pl.BlockSpec(memory_space=pltpu.VMEM)
    return pl.pallas_call(
        score_kernel,
        out_shape=(
            jax.ShapeDtypeStruct((32, 256, 128), jnp.float32),
            jax.ShapeDtypeStruct((16, 8, 256), jnp.float32),
        ),
        in_specs=[vmem, vmem, pl.BlockSpec(memory_space=pltpu.MemorySpace.HBM)],
        out_specs=(vmem, vmem),
        scratch_shapes=[
            pltpu.VMEM((32, 256, 128), jnp.float32),
            pltpu.VMEM((4096, 768), jnp.bfloat16),
            pltpu.SemaphoreType.DMA((8,)),
        ],
        compiler_params=limit(28),
        cost_estimate=cost(8),
    )(asked, count, slab)


def pull_kernel(me_ref, stat_ref, weight_ref, share_ref, slab_ref, out_ref, factor, total):
    step = pl.program_id(0)

    @pl.when(step == 0)
    def _():
        stats = stat_ref[...]
        tops, masses = stats[:, 0], stats[:, 1]
        best = jnp.max(tops, axis=0, keepdims=True)
        mass = jnp.sum(jnp.exp(tops - best) * masses, axis=0, keepdims=True)
        mine = stat_ref[me_ref[0]][0:1]
        line = loss_scale * jnp.exp(mine - best) / mass
        factor[...] = jnp.transpose(jnp.broadcast_to(line, (128, 256)))
        total[...] = jnp.zeros_like(total)

    coef = jnp.concatenate(
        [weight_ref[i] * factor[...] - loss_scale * share_ref[i] for i in range(4)], axis=1
    )
    both = jnp.concatenate(halves(coef), axis=0)
    got = jnp.dot(both, slab_ref[...], preferred_element_type=jnp.float32)
    total[...] += got[:256] + got[256:]

    @pl.when(step == 7)
    def _():
        out_ref[...] = total[...].astype(jnp.bfloat16)


def pull(me, stats, weight, share, slab):
    quarter = pl.BlockSpec((4, 256, 128), lambda j, me: (j, 0, 0))
    return pl.pallas_call(
        pull_kernel,
        grid_spec=pltpu.PrefetchScalarGridSpec(
            num_scalar_prefetch=1,
            grid=(8,),
            in_specs=[whole(16, 8, 256), quarter, quarter, pl.BlockSpec((512, 768), lambda j, me: (j, 0))],
            out_specs=whole(256, 768),
            scratch_shapes=[pltpu.VMEM((256, 128), jnp.float32), pltpu.VMEM((256, 768), jnp.float32)],
        ),
        out_shape=jax.ShapeDtypeStruct((256, 768), jnp.bfloat16),
        compiler_params=limit(16),
        cost_estimate=cost(5),
    )(me, stats, weight, share, slab)


def resid_kernel(came_ref, normed_ref, rstd_ref, vectors_ref, resid_grad_ref, out_grad_ref, ups):
    step = pl.program_id(0)

    @pl.when(step == 0)
    def _():
        ups[...] = jnp.sum(came_ref[...].astype(jnp.float32), axis=0) * (1 / 64) * vectors_ref[:, 768:1536]

    for q in range(4):
        up = ups[pl.ds(step * 4 + q, 1), :]
        rows = slice(q * 64, q * 64 + 64)
        normed = normed_ref[rows, :]
        along = jnp.mean(up * normed, axis=-1, keepdims=True)
        grad = (up - jnp.mean(up, axis=-1, keepdims=True) - normed * along) * rstd_ref[rows, :]
        resid_grad_ref[rows, :] = grad
        out_grad_ref[rows, :] = grad.astype(jnp.bfloat16)


def resid_gradient(came, normed, rstd, vectors):
    rows = pl.BlockSpec((256, 768), lambda j: (j, 0))
    return pl.pallas_call(
        resid_kernel,
        grid=(4,),
        in_specs=[
            whole(16, 16, 768),
            rows,
            pl.BlockSpec((256, 1), lambda j: (j, 0)),
            whole(1, 3072),
        ],
        out_specs=(rows, rows),
        out_shape=(
            jax.ShapeDtypeStruct((1024, 768), jnp.float32),
            jax.ShapeDtypeStruct((1024, 768), jnp.bfloat16),
        ),
        scratch_shapes=[pltpu.VMEM((16, 768), jnp.float32)],
        compiler_params=limit(16),
        cost_estimate=cost(2),
    )(came, normed, rstd, vectors)


def weight_kernel(place_ref, left_ref, right_ref, away_ref, kept_ref):
    got = columns_dot(left_ref[...], right_ref[...])
    core = place_ref[0]
    for mine in range(2):

        @pl.when(core == mine)
        def _():
            kept_ref[0] = got[mine * 384 : mine * 384 + 384].astype(jnp.bfloat16)
            away_ref[0] = got[384 - mine * 384 : 768 - mine * 384].astype(jnp.bfloat16)


def weight_sums(place, left, right):
    return pl.pallas_call(
        weight_kernel,
        grid_spec=pltpu.PrefetchScalarGridSpec(
            num_scalar_prefetch=1,
            grid=(4,),
            in_specs=[pl.BlockSpec((1024, 768), lambda j, place: (0, j)), whole(1024, 768)],
            out_specs=(pl.BlockSpec((1, 384, 768), lambda j, place: (j, 0, 0)),) * 2,
        ),
        out_shape=(jax.ShapeDtypeStruct((4, 384, 768), jnp.bfloat16),) * 2,
        compiler_params=limit(56),
        cost_estimate=cost(40),
    )(place, left, right)


def second_kernel(place_ref, kept_ref, came_ref, carry_ref, own_ref, one_ref, three_ref, two_ref, carried_ref):
    for out, step in ((own_ref, 0), (one_ref, 1), (three_ref, 3), (two_ref, 2)):
        at = (place_ref[1] + step) % 4
        out[...] = (kept_ref[at].astype(jnp.float32) + came_ref[at].astype(jnp.float32)).astype(out.dtype)


def second_pair(place, kept, came, carry):
    block = lambda j, place: (0, j, 0)
    piece = pl.BlockSpec((96, 768), lambda j, place: (j, 0))
    return pl.pallas_call(
        second_kernel,
        grid_spec=pltpu.PrefetchScalarGridSpec(
            num_scalar_prefetch=1,
            grid=(4,),
            in_specs=[pl.BlockSpec((4, 96, 768), block), pl.BlockSpec((4, 96, 768), block), anywhere],
            out_specs=(piece,) * 4 + (anywhere,),
        ),
        out_shape=(jax.ShapeDtypeStruct((384, 768), jnp.float32),)
        + (jax.ShapeDtypeStruct((384, 768), jnp.bfloat16),) * 3
        + (jax.ShapeDtypeStruct(carry.shape, carry.dtype),),
        input_output_aliases={3: 4},
        compiler_params=limit(56),
        cost_estimate=cost(5),
    )(place, kept, came, carry)


def first_kernel(place_ref, kept_ref, came_ref, *refs):
    own_ref, one_ref, three_ref, two_ref, right_ref = refs[-6:-1]
    for out, step in ((own_ref, 0), (one_ref, 1), (three_ref, 3), (two_ref, 2)):
        at = (place_ref[1] + step) % 4
        got = kept_ref[at, :, :384].astype(jnp.float32) + came_ref[at, :, :384].astype(jnp.float32)
        out[...] = got.astype(out.dtype)
    right = [
        kept_ref[y, :, 384:].astype(jnp.float32) + came_ref[y, :, 384:].astype(jnp.float32) for y in range(4)
    ]
    for i in range(4):
        rows = slice(i * 24, i * 24 + 24)
        right_ref[i] = jnp.concatenate([part[rows] for part in right], axis=0).astype(jnp.bfloat16)


def first_pair(place, kept, came, carry, *after):
    block = lambda j, place: (0, j, 0)
    piece = pl.BlockSpec((96, 384), lambda j, place: (j, 0))
    return pl.pallas_call(
        first_kernel,
        grid_spec=pltpu.PrefetchScalarGridSpec(
            num_scalar_prefetch=1,
            grid=(4,),
            in_specs=[pl.BlockSpec((4, 96, 768), block), pl.BlockSpec((4, 96, 768), block)]
            + [anywhere] * (1 + len(after)),
            out_specs=(piece,) * 4 + (pl.BlockSpec((4, 96, 384), lambda j, place: (j, 0, 0)), anywhere),
        ),
        out_shape=(jax.ShapeDtypeStruct((384, 384), jnp.float32),)
        + (jax.ShapeDtypeStruct((384, 384), jnp.bfloat16),) * 3
        + (
            jax.ShapeDtypeStruct((16, 96, 384), jnp.bfloat16),
            jax.ShapeDtypeStruct(carry.shape, carry.dtype),
        ),
        input_output_aliases={3: 5},
        compiler_params=limit(56),
        cost_estimate=cost(5),
    )(place, kept, came, carry, *after)


def hold(carry, *after):
    return pl.pallas_call(
        lambda *refs: None,
        in_specs=[anywhere] * (1 + len(after)),
        out_specs=anywhere,
        out_shape=jax.ShapeDtypeStruct(carry.shape, carry.dtype),
        input_output_aliases={0: 0},
        compiler_params=limit(56),
        cost_estimate=cost(1),
    )(carry, *after)


def mark_kernel(own_ref, out_ref):
    out_ref[...] = own_ref[...]


def mark(own):
    tile = pl.BlockSpec((8, 128), lambda j: (0, 0))
    return pl.pallas_call(
        mark_kernel,
        grid=(1,),
        in_specs=[tile],
        out_specs=tile,
        out_shape=jax.ShapeDtypeStruct((8, 128), jnp.float32),
        compiler_params=limit(56),
        cost_estimate=cost(100),
    )(own)


def left_kernel(*refs):
    out_ref = refs[-1]
    for parts, cols in ((refs[:4], slice(0, 384)), (refs[4:8], slice(384, 1152))):
        total = parts[0][...]
        for part in parts[1:]:
            total = total + part[...].astype(jnp.float32)
        out_ref[:, cols] = total.astype(jnp.bfloat16)


def left_sums(first, second, after):
    narrow, wide = (pl.BlockSpec((96, n), lambda j: (j, 0)) for n in (384, 768))
    return pl.pallas_call(
        left_kernel,
        grid=(4,),
        in_specs=[narrow] * 4 + [wide] * 4 + [anywhere],
        out_specs=pl.BlockSpec((96, 1152), lambda j: (j, 0)),
        out_shape=jax.ShapeDtypeStruct((384, 1152), jnp.bfloat16),
        compiler_params=limit(56),
        cost_estimate=cost(2),
    )(*first, *second, after)


def right_kernel(y_ref, came_ref, after_ref, own_ref, one_ref, three_ref, two_ref, total):
    total[...] = jnp.sum(came_ref[...].astype(jnp.float32), axis=0)
    for out, step in ((own_ref, 0), (one_ref, 1), (three_ref, 3), (two_ref, 2)):
        at = (y_ref[0] + step) % 4
        out[...] = total[pl.ds(pl.multiple_of(at * 24, 8), 24), :]


def right_sums(y, came, after):
    vmem = pl.BlockSpec(memory_space=pltpu.VMEM)
    return pl.pallas_call(
        right_kernel,
        in_specs=[pl.BlockSpec(memory_space=pltpu.SMEM), vmem, anywhere],
        out_specs=(vmem,) * 4,
        out_shape=(jax.ShapeDtypeStruct((24, 384), jnp.float32),) * 4,
        scratch_shapes=[pltpu.VMEM((96, 384), jnp.float32)],
        compiler_params=limit(8),
        cost_estimate=cost(1),
    )(y, came, after)


def last_kernel(devices, left_ref, own_ref, one_ref, three_ref, two_ref, out_ref):
    left = jnp.sum(left_ref[...].astype(jnp.float32), axis=0) / devices
    right = (own_ref[...] + one_ref[...] + three_ref[...] + two_ref[...]) / devices
    out_ref[:, :384] = left[:, :384]
    out_ref[:, 384:768] = right
    out_ref[:, 768:] = left[:, 384:]


def last_sums(devices, left, *right):
    vmem = pl.BlockSpec(memory_space=pltpu.VMEM)
    return pl.pallas_call(
        lambda *refs: last_kernel(devices, *refs),
        in_specs=[vmem] * 5,
        out_specs=vmem,
        out_shape=jax.ShapeDtypeStruct((24, 1536), jnp.float32),
        compiler_params=limit(8),
        cost_estimate=cost(1),
    )(left, *right)


def body(
    tokens, w_in, bias_in, w_out, bias_out, gain, shift, slab, owners, offsets, reader_weights
):
    devices = lax.axis_size("query") * lax.axis_size("index")
    me = lax.axis_index("index")[None]
    y = lax.axis_index("query") // 2
    core = lax.axis_index("query") % 2
    place = jnp.stack([core, y])

    asked = exchange(table(owners[..., 0], offsets, reader_weights))
    vectors = jnp.concatenate([bias_out, gain, shift, jnp.zeros_like(shift)]).reshape(1, 3072)
    hidden, slopes, normed, rstd, ask = forward(tokens, w_in, bias_in, w_out, vectors)
    count, share = picks(me, asked, rstd)
    weight, stat = score(exchange(ask), count, slab)
    partial = pull(me, exchange(stat), weight, share, slab)
    came = exchange(partial.reshape(16, 16, 768))
    resid_grad, out_grad = resid_gradient(came, normed, rstd, vectors)

    def round_y(own, *pieces):
        return [own] + [shifted(piece, 0, step) for piece, step in zip(pieces, (1, 3, 2))]

    away, kept = weight_sums(place, hidden, out_grad)
    pre_grad = (
        jnp.dot(out_grad, w_out.T, preferred_element_type=jnp.float32) * slopes.astype(jnp.float32)
    ).astype(jnp.bfloat16)
    *second, pre_grad = second_pair(place, kept, shifted(away, 1, 0), pre_grad)
    second = round_y(*second)
    away, kept = weight_sums(place, pre_grad, tokens)
    away = hold(away, second[1], second[2])
    *first, packed, pre_grad = first_pair(
        place, kept, shifted(away, 1, 0), pre_grad, mark(second[0])
    )
    first = round_y(*first)
    right = exchange(packed)
    token_grads = (
        resid_grad + jnp.dot(pre_grad, w_in.T, preferred_element_type=jnp.float32)
    ).astype(jnp.bfloat16)

    left = exchange(left_sums(first, second, token_grads).reshape(16, 24, 1152))
    own, one, three, two = right_sums(y[None], right, token_grads)
    right = round_y(own, one, three, two)
    return (token_grads, last_sums(devices, left, *right))


def solution(mesh):
    placed = (
        P(("query", "index"), None),
        P(),
        P(),
        P(),
        P(),
        P(),
        P(),
        P("index", None),
        P(("query", "index"), None, None),
        P(("query", "index"), None),
        P(("query", "index"), None),
    )
    return jax.shard_map(
        body,
        mesh=mesh,
        in_specs=placed,
        out_specs=(P(("query", "index"), None), P(("query", "index"), None)),
        check_vma=False,
    )
```

```python
import jax
import jax.numpy as jnp
from jax import lax
from jax.experimental import pallas as pl
from jax.experimental.pallas import tpu as pltpu
from jax.sharding import PartitionSpec as P

loss_scale = 256.0
norm_eps = 1e-12
every = ("query", "index")
MIB = 1 << 20
low = -1e30


def limit(mib):
    return pltpu.CompilerParams(vmem_limit_bytes=mib * MIB)


def cost(us):
    return pl.CostEstimate(flops=us * 1_000_000_000, bytes_accessed=1000, transcendentals=0)
anywhere = pl.BlockSpec(memory_space=pl.ANY)


def halves(value):
    first = value.astype(jnp.bfloat16)
    return first, (value - first.astype(jnp.float32)).astype(jnp.bfloat16)


def dot_rows(left, right):
    return lax.dot_general(left, right, (((1,), (1,)), ((), ())), preferred_element_type=jnp.float32)


def columns_dot(left, right):
    return lax.dot_general(left, right, (((0,), (0,)), ((), ())), preferred_element_type=jnp.float32)


def exchange(value):
    return lax.all_to_all(value, "index", 0, 0, tiled=True)


def shifted(value, core, along_y):
    pairs = []
    for query in range(8):
        y, c = query // 2, query % 2
        to = ((y + along_y) % 4) * 2 + (c + core) % 2
        pairs += [(query * 16 + i, to * 16 + i) for i in range(16)]
    return lax.ppermute(value, every, pairs)


def whole(*shape):
    return pl.BlockSpec(shape, lambda *_: (0,) * len(shape))


def slope(pre):
    square = pre * pre
    bend = jnp.tanh(pre * (0.7978845608028654 + 0.035677408136300125 * square))
    share = 0.5 + 0.5 * bend
    value = pre * share
    grad = share + (value - value * share) * (1.5957691216057308 + 0.21406444881780074 * square)
    return value, grad


def forward_kernel(
    tokens_ref, w_in_ref, bias_in_ref, w_out_ref, vectors_ref,
    hidden_ref, slope_ref, normed_ref, rstd_ref, ask_ref, resid, query,
):
    step = pl.program_id(0)

    @pl.when(step == 0)
    def _():
        resid[...] = tokens_ref[...].astype(jnp.float32) + vectors_ref[:, :768]

    for part in range(4):
        rows = slice(part * 256, part * 256 + 256)
        pre = jnp.dot(tokens_ref[rows, :], w_in_ref[...], preferred_element_type=jnp.float32) + bias_in_ref[...]
        value, grad = slope(pre)
        value = value.astype(jnp.bfloat16)
        hidden_ref[rows, :] = value
        slope_ref[rows, :] = grad.astype(jnp.bfloat16)
        resid[rows, :] += jnp.dot(value, w_out_ref[...], preferred_element_type=jnp.float32)

    @pl.when(step == pl.num_programs(0) - 1)
    def _():
        for q in range(16):
            rows = slice(q * 64, q * 64 + 64)
            here = resid[rows, :]
            away = here - jnp.mean(here, axis=-1, keepdims=True)
            rstd = lax.rsqrt(jnp.mean(away * away, axis=-1, keepdims=True) + norm_eps)
            normed = away * rstd
            normed_ref[rows, :] = normed
            rstd_ref[rows, :] = rstd
            query[q : q + 1, :] = (
                jnp.sum(normed, axis=0, keepdims=True) * (1 / 64) * vectors_ref[:, 768:1536] + vectors_ref[:, 1536:2304]
            )
        upper, lower = halves(query[...])
        for to in range(16):
            ask_ref[to, :, :768] = upper
            ask_ref[to, :, 768:] = lower


def forward(tokens, w_in, bias_in, w_out, vectors):
    block = 512
    units = pl.BlockSpec((1024, block), lambda j: (0, j))
    return pl.pallas_call(
        forward_kernel,
        grid=(3072 // block,),
        in_specs=[
            whole(1024, 768),
            pl.BlockSpec((768, block), lambda j: (0, j)),
            pl.BlockSpec((1, block), lambda j: (0, j)),
            pl.BlockSpec((block, 768), lambda j: (j, 0)),
            whole(1, 3072),
        ],
        out_specs=(units, units, whole(1024, 768), whole(1024, 1), whole(16, 16, 1536)),
        out_shape=(
            jax.ShapeDtypeStruct((1024, 3072), jnp.bfloat16),
            jax.ShapeDtypeStruct((1024, 3072), jnp.bfloat16),
            jax.ShapeDtypeStruct((1024, 768), jnp.float32),
            jax.ShapeDtypeStruct((1024, 1), jnp.float32),
            jax.ShapeDtypeStruct((16, 16, 1536), jnp.bfloat16),
        ),
        scratch_shapes=[pltpu.VMEM((1024, 768), jnp.float32), pltpu.VMEM((16, 768), jnp.float32)],
        compiler_params=limit(56),
        cost_estimate=cost(20),
    )(tokens, w_in, bias_in.reshape(1, -1), w_out, vectors)


def table_kernel(owner_ref, offset_ref, weight_ref, out_ref):
    weight = weight_ref[...]
    target = weight / jnp.sum(weight, axis=-1, keepdims=True)
    offset = offset_ref[...]
    upper, lower = halves(target)
    fields = [
        owner_ref[...].astype(jnp.float32),
        (offset // 128).astype(jnp.float32),
        (offset % 128).astype(jnp.float32),
        upper.astype(jnp.float32),
        lower.astype(jnp.float32),
    ]
    rows = [
        jnp.concatenate([field[g * 8 + i : g * 8 + i + 1] for i in range(8)], axis=1)
        for field in fields
        for g in range(2)
    ]
    rows = jnp.concatenate(rows + [jnp.zeros((6, 512), jnp.float32)], axis=0).astype(jnp.bfloat16)
    for to in range(16):
        out_ref[to] = rows


def table(owners, offsets, reader_weights):
    vmem = pl.BlockSpec(memory_space=pltpu.VMEM)
    return pl.pallas_call(
        table_kernel,
        in_specs=[vmem] * 3,
        out_specs=vmem,
        out_shape=jax.ShapeDtypeStruct((16, 16, 512), jnp.bfloat16),
        compiler_params=limit(56),
        cost_estimate=cost(1),
    )(owners, offsets, reader_weights)


def picks_kernel(me_ref, table_ref, after_ref, count_ref, share_ref):
    me = me_ref[0].astype(jnp.float32)
    turn = (lax.broadcasted_iota(jnp.int32, (1, 512), 1) // 64).astype(jnp.float32)
    row = lax.broadcasted_iota(jnp.int32, (256, 512), 0).astype(jnp.float32)
    line = lax.broadcasted_iota(jnp.int32, (128, 512), 0).astype(jnp.float32)

    def source(s, carry):
        meta = table_ref[s].astype(jnp.float32)
        counts = []
        for g in range(2):
            owner, high, spot, upper, lower = [meta[2 * f + g : 2 * f + g + 1] for f in range(5)]
            key = jnp.where(owner == me, high * 8.0 + turn, -1.0)
            left = jnp.where(row == key, 1.0, 0.0).astype(jnp.bfloat16)
            hit = line == spot
            right = jnp.concatenate(
                [jnp.where(hit, 1.0, 0.0), jnp.where(hit, upper, 0.0), jnp.where(hit, lower, 0.0)], axis=0
            ).astype(jnp.bfloat16)
            out = dot_rows(left, right)
            at = pl.ds(pl.multiple_of(s * 16 + g * 8, 8), 8)
            counts.append(out[:, :128].reshape(32, 8, 128))
            share_ref[:, at, :] = (out[:, 128:256] + out[:, 256:]).reshape(32, 8, 128)
        at = pl.ds(pl.multiple_of(s * 16, 16), 16)
        count_ref[:, at, :] = jnp.concatenate(counts, axis=1).astype(jnp.bfloat16)
        return carry

    lax.fori_loop(0, 16, source, 0, unroll=2)


def picks(me, asked, after):
    vmem = pl.BlockSpec(memory_space=pltpu.VMEM)
    return pl.pallas_call(
        picks_kernel,
        out_shape=(
            jax.ShapeDtypeStruct((32, 256, 128), jnp.bfloat16),
            jax.ShapeDtypeStruct((32, 256, 128), jnp.float32),
        ),
        in_specs=[pl.BlockSpec(memory_space=pltpu.SMEM), vmem, anywhere],
        out_specs=(vmem, vmem),
        compiler_params=limit(24),
        cost_estimate=cost(10),
    )(me, asked, after)


def score_kernel(ask_ref, count_ref, slab, weight_ref, stat_ref, scores):
    both = jnp.concatenate(
        [ask_ref[:, :, :768].reshape(256, 768), ask_ref[:, :, 768:].reshape(256, 768)], axis=0
    )
    top = jnp.full((256, 128), low, jnp.float32)
    for block in range(8):
        got = dot_rows(both, slab[block * 512 : block * 512 + 512])
        got = got[:256] + got[256:]
        for i in range(4):
            part = got[:, i * 128 : i * 128 + 128]
            scores[block * 4 + i] = part
            top = jnp.maximum(top, jnp.where(count_ref[block * 4 + i].astype(jnp.float32) > 0, part, low))
    top = jnp.max(top, axis=1, keepdims=True)
    mass = jnp.zeros((256, 128), jnp.float32)
    for high in range(32):
        here = count_ref[high].astype(jnp.float32)
        part = jnp.where(here > 0, here * jnp.exp(jnp.minimum(scores[high] - top, 0.0)), 0.0)
        mass = mass + part
        weight_ref[high] = part
    mass = jnp.sum(mass, axis=1, keepdims=True)
    lane = lax.broadcasted_iota(jnp.int32, (256, 128), 1)
    stat = jnp.transpose(jnp.where(lane == 0, top, mass))[:8]
    for to in range(16):
        stat_ref[to] = stat


def score(asked, count, slab):
    vmem = pl.BlockSpec(memory_space=pltpu.VMEM)
    return pl.pallas_call(
        score_kernel,
        out_shape=(
            jax.ShapeDtypeStruct((32, 256, 128), jnp.float32),
            jax.ShapeDtypeStruct((16, 8, 256), jnp.float32),
        ),
        in_specs=[vmem, vmem, vmem],
        out_specs=(vmem, vmem),
        scratch_shapes=[pltpu.VMEM((32, 256, 128), jnp.float32)],
        compiler_params=limit(24),
        cost_estimate=cost(8),
    )(asked, count, slab)


def pull_kernel(me_ref, stat_ref, weight_ref, share_ref, slab_ref, out_ref, factor, total):
    step = pl.program_id(0)

    @pl.when(step == 0)
    def _():
        stats = stat_ref[...]
        tops, masses = stats[:, 0], stats[:, 1]
        best = jnp.max(tops, axis=0, keepdims=True)
        mass = jnp.sum(jnp.exp(tops - best) * masses, axis=0, keepdims=True)
        mine = stat_ref[me_ref[0]][0:1]
        line = loss_scale * jnp.exp(mine - best) / mass
        factor[...] = jnp.transpose(jnp.broadcast_to(line, (128, 256)))
        total[...] = jnp.zeros_like(total)

    coef = jnp.concatenate(
        [weight_ref[i] * factor[...] - loss_scale * share_ref[i] for i in range(4)], axis=1
    )
    both = jnp.concatenate(halves(coef), axis=0)
    got = jnp.dot(both, slab_ref[...], preferred_element_type=jnp.float32)
    total[...] += got[:256] + got[256:]

    @pl.when(step == 7)
    def _():
        out_ref[...] = total[...].astype(jnp.bfloat16)


def pull(me, stats, weight, share, slab):
    quarter = pl.BlockSpec((4, 256, 128), lambda j, me: (j, 0, 0))
    return pl.pallas_call(
        pull_kernel,
        grid_spec=pltpu.PrefetchScalarGridSpec(
            num_scalar_prefetch=1,
            grid=(8,),
            in_specs=[whole(16, 8, 256), quarter, quarter, pl.BlockSpec((512, 768), lambda j, me: (j, 0))],
            out_specs=whole(256, 768),
            scratch_shapes=[pltpu.VMEM((256, 128), jnp.float32), pltpu.VMEM((256, 768), jnp.float32)],
        ),
        out_shape=jax.ShapeDtypeStruct((256, 768), jnp.bfloat16),
        compiler_params=limit(16),
        cost_estimate=cost(5),
    )(me, stats, weight, share, slab)


def resid_kernel(came_ref, normed_ref, rstd_ref, vectors_ref, resid_grad_ref, out_grad_ref, ups):
    step = pl.program_id(0)

    @pl.when(step == 0)
    def _():
        ups[...] = jnp.sum(came_ref[...].astype(jnp.float32), axis=0) * (1 / 64) * vectors_ref[:, 768:1536]

    for q in range(4):
        up = ups[pl.ds(step * 4 + q, 1), :]
        rows = slice(q * 64, q * 64 + 64)
        normed = normed_ref[rows, :]
        along = jnp.mean(up * normed, axis=-1, keepdims=True)
        grad = (up - jnp.mean(up, axis=-1, keepdims=True) - normed * along) * rstd_ref[rows, :]
        resid_grad_ref[rows, :] = grad
        out_grad_ref[rows, :] = grad.astype(jnp.bfloat16)


def resid_gradient(came, normed, rstd, vectors):
    rows = pl.BlockSpec((256, 768), lambda j: (j, 0))
    return pl.pallas_call(
        resid_kernel,
        grid=(4,),
        in_specs=[
            whole(16, 16, 768),
            rows,
            pl.BlockSpec((256, 1), lambda j: (j, 0)),
            whole(1, 3072),
        ],
        out_specs=(rows, rows),
        out_shape=(
            jax.ShapeDtypeStruct((1024, 768), jnp.float32),
            jax.ShapeDtypeStruct((1024, 768), jnp.bfloat16),
        ),
        scratch_shapes=[pltpu.VMEM((16, 768), jnp.float32)],
        compiler_params=limit(16),
        cost_estimate=cost(2),
    )(came, normed, rstd, vectors)


def weight_kernel(place_ref, left_ref, right_ref, away_ref, kept_ref):
    got = columns_dot(left_ref[...], right_ref[...])
    core = place_ref[0]
    for mine in range(2):

        @pl.when(core == mine)
        def _():
            kept_ref[0] = got[mine * 384 : mine * 384 + 384].astype(jnp.bfloat16)
            away_ref[0] = got[384 - mine * 384 : 768 - mine * 384].astype(jnp.bfloat16)


def weight_sums(place, left, right):
    return pl.pallas_call(
        weight_kernel,
        grid_spec=pltpu.PrefetchScalarGridSpec(
            num_scalar_prefetch=1,
            grid=(4,),
            in_specs=[pl.BlockSpec((1024, 768), lambda j, place: (0, j)), whole(1024, 768)],
            out_specs=(pl.BlockSpec((1, 384, 768), lambda j, place: (j, 0, 0)),) * 2,
        ),
        out_shape=(jax.ShapeDtypeStruct((4, 384, 768), jnp.bfloat16),) * 2,
        compiler_params=limit(24),
        cost_estimate=cost(40),
    )(place, left, right)


def second_kernel(place_ref, kept_ref, came_ref, carry_ref, own_ref, one_ref, three_ref, two_ref, carried_ref):
    for out, step in ((own_ref, 0), (one_ref, 1), (three_ref, 3), (two_ref, 2)):
        at = (place_ref[1] + step) % 4
        out[...] = (kept_ref[at].astype(jnp.float32) + came_ref[at].astype(jnp.float32)).astype(out.dtype)


def second_pair(place, kept, came, carry):
    block = lambda j, place: (0, j, 0)
    piece = pl.BlockSpec((96, 768), lambda j, place: (j, 0))
    return pl.pallas_call(
        second_kernel,
        grid_spec=pltpu.PrefetchScalarGridSpec(
            num_scalar_prefetch=1,
            grid=(4,),
            in_specs=[pl.BlockSpec((4, 96, 768), block), pl.BlockSpec((4, 96, 768), block), anywhere],
            out_specs=(piece,) * 4 + (anywhere,),
        ),
        out_shape=(jax.ShapeDtypeStruct((384, 768), jnp.float32),)
        + (jax.ShapeDtypeStruct((384, 768), jnp.bfloat16),) * 3
        + (jax.ShapeDtypeStruct(carry.shape, carry.dtype),),
        input_output_aliases={3: 4},
        compiler_params=limit(16),
        cost_estimate=cost(5),
    )(place, kept, came, carry)


def first_kernel(place_ref, kept_ref, came_ref, *refs):
    own_ref, one_ref, three_ref, two_ref, right_ref = refs[-6:-1]
    for out, step in ((own_ref, 0), (one_ref, 1), (three_ref, 3), (two_ref, 2)):
        at = (place_ref[1] + step) % 4
        got = kept_ref[at, :, :384].astype(jnp.float32) + came_ref[at, :, :384].astype(jnp.float32)
        out[...] = got.astype(out.dtype)
    right = [
        kept_ref[y, :, 384:].astype(jnp.float32) + came_ref[y, :, 384:].astype(jnp.float32) for y in range(4)
    ]
    for i in range(4):
        rows = slice(i * 24, i * 24 + 24)
        right_ref[i] = jnp.concatenate([part[rows] for part in right], axis=0).astype(jnp.bfloat16)


def first_pair(place, kept, came, carry, *after):
    block = lambda j, place: (0, j, 0)
    piece = pl.BlockSpec((96, 384), lambda j, place: (j, 0))
    return pl.pallas_call(
        first_kernel,
        grid_spec=pltpu.PrefetchScalarGridSpec(
            num_scalar_prefetch=1,
            grid=(4,),
            in_specs=[pl.BlockSpec((4, 96, 768), block), pl.BlockSpec((4, 96, 768), block)]
            + [anywhere] * (1 + len(after)),
            out_specs=(piece,) * 4 + (pl.BlockSpec((4, 96, 384), lambda j, place: (j, 0, 0)), anywhere),
        ),
        out_shape=(jax.ShapeDtypeStruct((384, 384), jnp.float32),)
        + (jax.ShapeDtypeStruct((384, 384), jnp.bfloat16),) * 3
        + (
            jax.ShapeDtypeStruct((16, 96, 384), jnp.bfloat16),
            jax.ShapeDtypeStruct(carry.shape, carry.dtype),
        ),
        input_output_aliases={3: 5},
        compiler_params=limit(16),
        cost_estimate=cost(5),
    )(place, kept, came, carry, *after)


def hold(carry, *after):
    return pl.pallas_call(
        lambda *refs: None,
        in_specs=[anywhere] * (1 + len(after)),
        out_specs=anywhere,
        out_shape=jax.ShapeDtypeStruct(carry.shape, carry.dtype),
        input_output_aliases={0: 0},
        compiler_params=limit(4),
        cost_estimate=cost(1),
    )(carry, *after)


def mark_kernel(own_ref, out_ref):
    out_ref[...] = own_ref[...]


def mark(own):
    tile = pl.BlockSpec((8, 128), lambda j: (0, 0))
    return pl.pallas_call(
        mark_kernel,
        grid=(1,),
        in_specs=[tile],
        out_specs=tile,
        out_shape=jax.ShapeDtypeStruct((8, 128), jnp.float32),
        compiler_params=limit(4),
        cost_estimate=cost(100),
    )(own)


def left_kernel(*refs):
    out_ref = refs[-1]
    for parts, cols in ((refs[:4], slice(0, 384)), (refs[4:8], slice(384, 1152))):
        total = parts[0][...]
        for part in parts[1:]:
            total = total + part[...].astype(jnp.float32)
        out_ref[:, cols] = total.astype(jnp.bfloat16)


def left_sums(first, second, after):
    narrow, wide = (pl.BlockSpec((96, n), lambda j: (j, 0)) for n in (384, 768))
    return pl.pallas_call(
        left_kernel,
        grid=(4,),
        in_specs=[narrow] * 4 + [wide] * 4 + [anywhere],
        out_specs=pl.BlockSpec((96, 1152), lambda j: (j, 0)),
        out_shape=jax.ShapeDtypeStruct((384, 1152), jnp.bfloat16),
        compiler_params=limit(16),
        cost_estimate=cost(2),
    )(*first, *second, after)


def right_kernel(y_ref, came_ref, after_ref, own_ref, one_ref, three_ref, two_ref, total):
    total[...] = jnp.sum(came_ref[...].astype(jnp.float32), axis=0)
    for out, step in ((own_ref, 0), (one_ref, 1), (three_ref, 3), (two_ref, 2)):
        at = (y_ref[0] + step) % 4
        out[...] = total[pl.ds(pl.multiple_of(at * 24, 8), 24), :]


def right_sums(y, came, after):
    vmem = pl.BlockSpec(memory_space=pltpu.VMEM)
    return pl.pallas_call(
        right_kernel,
        in_specs=[pl.BlockSpec(memory_space=pltpu.SMEM), vmem, anywhere],
        out_specs=(vmem,) * 4,
        out_shape=(jax.ShapeDtypeStruct((24, 384), jnp.float32),) * 4,
        scratch_shapes=[pltpu.VMEM((96, 384), jnp.float32)],
        compiler_params=limit(8),
        cost_estimate=cost(1),
    )(y, came, after)


def last_kernel(devices, left_ref, own_ref, one_ref, three_ref, two_ref, out_ref):
    left = jnp.sum(left_ref[...].astype(jnp.float32), axis=0) / devices
    right = (own_ref[...] + one_ref[...] + three_ref[...] + two_ref[...]) / devices
    out_ref[:, :384] = left[:, :384]
    out_ref[:, 384:768] = right
    out_ref[:, 768:] = left[:, 384:]


def last_sums(devices, left, *right):
    vmem = pl.BlockSpec(memory_space=pltpu.VMEM)
    return pl.pallas_call(
        lambda *refs: last_kernel(devices, *refs),
        in_specs=[vmem] * 5,
        out_specs=vmem,
        out_shape=jax.ShapeDtypeStruct((24, 1536), jnp.float32),
        compiler_params=limit(8),
        cost_estimate=cost(1),
    )(left, *right)


def body(
    tokens, w_in, bias_in, w_out, bias_out, gain, shift, slab, owners, offsets, reader_weights
):
    devices = lax.axis_size("query") * lax.axis_size("index")
    me = lax.axis_index("index")[None]
    y = lax.axis_index("query") // 2
    core = lax.axis_index("query") % 2
    place = jnp.stack([core, y])

    asked = exchange(table(owners[..., 0], offsets, reader_weights))
    vectors = jnp.concatenate([bias_out, gain, shift, jnp.zeros_like(shift)]).reshape(1, 3072)
    hidden, slopes, normed, rstd, ask = forward(tokens, w_in, bias_in, w_out, vectors)
    count, share = picks(me, asked, rstd)
    weight, stat = score(exchange(ask), count, slab)
    partial = pull(me, exchange(stat), weight, share, slab)
    came = exchange(partial.reshape(16, 16, 768))
    resid_grad, out_grad = resid_gradient(came, normed, rstd, vectors)

    def round_y(own, *pieces):
        return [own] + [shifted(piece, 0, step) for piece, step in zip(pieces, (1, 3, 2))]

    away, kept = weight_sums(place, hidden, out_grad)
    *second, out_grad = second_pair(place, kept, shifted(away, 1, 0), out_grad)
    second = round_y(*second)
    pre_grad = (
        jnp.dot(out_grad, w_out.T, preferred_element_type=jnp.float32) * slopes.astype(jnp.float32)
    ).astype(jnp.bfloat16)
    away, kept = weight_sums(place, pre_grad, tokens)
    away = hold(away, second[1], second[2])
    *first, packed, pre_grad = first_pair(
        place, kept, shifted(away, 1, 0), pre_grad, mark(second[0])
    )
    first = round_y(*first)
    right = exchange(packed)
    token_grads = (
        resid_grad + jnp.dot(pre_grad, w_in.T, preferred_element_type=jnp.float32)
    ).astype(jnp.bfloat16)

    left = exchange(left_sums(first, second, token_grads).reshape(16, 24, 1152))
    own, one, three, two = right_sums(y[None], right, token_grads)
    right = round_y(own, one, three, two)
    return (token_grads, last_sums(devices, left, *right))


def solution(mesh):
    placed = (
        P(("query", "index"), None),
        P(),
        P(),
        P(),
        P(),
        P(),
        P(),
        P("index", None),
        P(("query", "index"), None, None),
        P(("query", "index"), None),
        P(("query", "index"), None),
    )
    return jax.shard_map(
        body,
        mesh=mesh,
        in_specs=placed,
        out_specs=(P(("query", "index"), None), P(("query", "index"), None)),
        check_vma=False,
    )
```

```python
import jax
import jax.numpy as jnp
from jax import lax
from jax.experimental import pallas as pl
from jax.experimental.pallas import tpu as pltpu
from jax.sharding import PartitionSpec as P

loss_scale = 256.0
norm_eps = 1e-12
every = ("query", "index")
MIB = 1 << 20
low = -1e30


def limit(mib):
    return pltpu.CompilerParams(vmem_limit_bytes=mib * MIB)


def cost(us):
    return pl.CostEstimate(flops=us * 1_000_000_000, bytes_accessed=1000, transcendentals=0)
anywhere = pl.BlockSpec(memory_space=pl.ANY)


def halves(value):
    first = value.astype(jnp.bfloat16)
    return first, (value - first.astype(jnp.float32)).astype(jnp.bfloat16)


def dot_rows(left, right):
    return lax.dot_general(left, right, (((1,), (1,)), ((), ())), preferred_element_type=jnp.float32)


def columns_dot(left, right):
    return lax.dot_general(left, right, (((0,), (0,)), ((), ())), preferred_element_type=jnp.float32)


def exchange(value):
    return lax.all_to_all(value, "index", 0, 0, tiled=True)


def shifted(value, core, along_y):
    pairs = []
    for query in range(8):
        y, c = query // 2, query % 2
        to = ((y + along_y) % 4) * 2 + (c + core) % 2
        pairs += [(query * 16 + i, to * 16 + i) for i in range(16)]
    return lax.ppermute(value, every, pairs)


def whole(*shape):
    return pl.BlockSpec(shape, lambda *_: (0,) * len(shape))


def slope(pre):
    square = pre * pre
    bend = jnp.tanh(pre * (0.7978845608028654 + 0.035677408136300125 * square))
    share = 0.5 + 0.5 * bend
    value = pre * share
    grad = share + (value - value * share) * (1.5957691216057308 + 0.21406444881780074 * square)
    return value, grad


def forward_kernel(
    tokens_ref, w_in_ref, bias_in_ref, w_out_ref, vectors_ref,
    hidden_ref, slope_ref, normed_ref, rstd_ref, ask_ref, resid, query, pres,
):
    step = pl.program_id(0)

    @pl.when(step == 0)
    def _():
        resid[...] = tokens_ref[...].astype(jnp.float32) + vectors_ref[:, :768]

    for part in range(10):
        if part < 8:
            rows = slice(part * 128, part * 128 + 128)
            pres[rows, :] = jnp.dot(tokens_ref[rows, :], w_in_ref[...], preferred_element_type=jnp.float32)
        if 1 <= part < 9:
            for start in range(part * 128 - 128, part * 128, 16):
                rows = slice(start, start + 16)
                value, grad = slope(pres[rows, :] + bias_in_ref[...])
                hidden_ref[rows, :] = value.astype(jnp.bfloat16)
                slope_ref[rows, :] = grad.astype(jnp.bfloat16)
        if 2 <= part:
            rows = slice(part * 128 - 256, part * 128 - 128)
            resid[rows, :] += jnp.dot(hidden_ref[rows, :], w_out_ref[...], preferred_element_type=jnp.float32)

    @pl.when(step == pl.num_programs(0) - 1)
    def _():
        for q in range(16):
            rows = slice(q * 64, q * 64 + 64)
            here = resid[rows, :]
            away = here - jnp.mean(here, axis=-1, keepdims=True)
            rstd = lax.rsqrt(jnp.mean(away * away, axis=-1, keepdims=True) + norm_eps)
            normed = away * rstd
            normed_ref[rows, :] = normed
            rstd_ref[rows, :] = rstd
            query[q : q + 1, :] = (
                jnp.sum(normed, axis=0, keepdims=True) * (1 / 64) * vectors_ref[:, 768:1536] + vectors_ref[:, 1536:2304]
            )
        upper, lower = halves(query[...])
        for to in range(16):
            ask_ref[to, :, :768] = upper
            ask_ref[to, :, 768:] = lower


def forward(tokens, w_in, bias_in, w_out, vectors):
    block = 512
    units = pl.BlockSpec((1024, block), lambda j: (0, j))
    return pl.pallas_call(
        forward_kernel,
        grid=(3072 // block,),
        in_specs=[
            whole(1024, 768),
            pl.BlockSpec((768, block), lambda j: (0, j)),
            pl.BlockSpec((1, block), lambda j: (0, j)),
            pl.BlockSpec((block, 768), lambda j: (j, 0)),
            whole(1, 3072),
        ],
        out_specs=(units, units, whole(1024, 768), whole(1024, 1), whole(16, 16, 1536)),
        out_shape=(
            jax.ShapeDtypeStruct((1024, 3072), jnp.bfloat16),
            jax.ShapeDtypeStruct((1024, 3072), jnp.bfloat16),
            jax.ShapeDtypeStruct((1024, 768), jnp.float32),
            jax.ShapeDtypeStruct((1024, 1), jnp.float32),
            jax.ShapeDtypeStruct((16, 16, 1536), jnp.bfloat16),
        ),
        scratch_shapes=[
            pltpu.VMEM((1024, 768), jnp.float32),
            pltpu.VMEM((16, 768), jnp.float32),
            pltpu.VMEM((1024, block), jnp.float32),
        ],
        compiler_params=limit(56),
        cost_estimate=cost(20),
    )(tokens, w_in, bias_in.reshape(1, -1), w_out, vectors)


def table_kernel(owner_ref, offset_ref, weight_ref, out_ref):
    weight = weight_ref[...]
    target = weight / jnp.sum(weight, axis=-1, keepdims=True)
    offset = offset_ref[...]
    upper, lower = halves(target)
    fields = [
        owner_ref[...].astype(jnp.float32),
        (offset // 128).astype(jnp.float32),
        (offset % 128).astype(jnp.float32),
        upper.astype(jnp.float32),
        lower.astype(jnp.float32),
    ]
    rows = [
        jnp.concatenate([field[g * 8 + i : g * 8 + i + 1] for i in range(8)], axis=1)
        for field in fields
        for g in range(2)
    ]
    rows = jnp.concatenate(rows + [jnp.zeros((6, 512), jnp.float32)], axis=0).astype(jnp.bfloat16)
    for to in range(16):
        out_ref[to] = rows


def table(owners, offsets, reader_weights):
    vmem = pl.BlockSpec(memory_space=pltpu.VMEM)
    return pl.pallas_call(
        table_kernel,
        in_specs=[vmem] * 3,
        out_specs=vmem,
        out_shape=jax.ShapeDtypeStruct((16, 16, 512), jnp.bfloat16),
        compiler_params=limit(56),
        cost_estimate=cost(1),
    )(owners, offsets, reader_weights)


def picks_kernel(place_ref, table_ref, after_ref, count_ref, share_ref):
    me = place_ref[2].astype(jnp.float32)
    turn = (lax.broadcasted_iota(jnp.int32, (1, 512), 1) // 64).astype(jnp.float32)
    row = lax.broadcasted_iota(jnp.int32, (256, 512), 0).astype(jnp.float32)
    line = lax.broadcasted_iota(jnp.int32, (128, 512), 0).astype(jnp.float32)

    def source(s, carry):
        meta = table_ref[s].astype(jnp.float32)
        counts = []
        for g in range(2):
            owner, high, spot, upper, lower = [meta[2 * f + g : 2 * f + g + 1] for f in range(5)]
            key = jnp.where(owner == me, high * 8.0 + turn, -1.0)
            left = jnp.where(row == key, 1.0, 0.0).astype(jnp.bfloat16)
            hit = line == spot
            right = jnp.concatenate(
                [jnp.where(hit, 1.0, 0.0), jnp.where(hit, upper, 0.0), jnp.where(hit, lower, 0.0)], axis=0
            ).astype(jnp.bfloat16)
            out = dot_rows(left, right)
            at = pl.ds(pl.multiple_of(s * 16 + g * 8, 8), 8)
            counts.append(out[:, :128].reshape(32, 8, 128))
            share_ref[:, at, :] = (out[:, 128:256] + out[:, 256:]).reshape(32, 8, 128)
        at = pl.ds(pl.multiple_of(s * 16, 16), 16)
        count_ref[:, at, :] = jnp.concatenate(counts, axis=1).astype(jnp.bfloat16)
        return carry

    lax.fori_loop(0, 16, source, 0, unroll=2)


def picks(place, asked, after):
    vmem = pl.BlockSpec(memory_space=pltpu.VMEM)
    return pl.pallas_call(
        picks_kernel,
        out_shape=(
            jax.ShapeDtypeStruct((32, 256, 128), jnp.bfloat16),
            jax.ShapeDtypeStruct((32, 256, 128), jnp.float32),
        ),
        in_specs=[pl.BlockSpec(memory_space=pltpu.SMEM), vmem, anywhere],
        out_specs=(vmem, vmem),
        compiler_params=limit(24),
        cost_estimate=cost(10),
    )(place, asked, after)


def score_kernel(ask_ref, count_ref, slab, weight_ref, stat_ref, scores):
    both = jnp.concatenate(
        [ask_ref[:, :, :768].reshape(256, 768), ask_ref[:, :, 768:].reshape(256, 768)], axis=0
    )
    top = jnp.full((256, 128), low, jnp.float32)
    for block in range(8):
        got = dot_rows(both, slab[block * 512 : block * 512 + 512])
        got = got[:256] + got[256:]
        for i in range(4):
            part = got[:, i * 128 : i * 128 + 128]
            scores[block * 4 + i] = part
            top = jnp.maximum(top, jnp.where(count_ref[block * 4 + i].astype(jnp.float32) > 0, part, low))
    top = jnp.max(top, axis=1, keepdims=True)
    mass = jnp.zeros((256, 128), jnp.float32)
    for high in range(32):
        here = count_ref[high].astype(jnp.float32)
        part = jnp.where(here > 0, here * jnp.exp(jnp.minimum(scores[high] - top, 0.0)), 0.0)
        mass = mass + part
        weight_ref[high] = part
    mass = jnp.sum(mass, axis=1, keepdims=True)
    lane = lax.broadcasted_iota(jnp.int32, (256, 128), 1)
    stat = jnp.transpose(jnp.where(lane == 0, top, mass))[:8]
    for to in range(16):
        stat_ref[to] = stat


def score(asked, count, slab):
    vmem = pl.BlockSpec(memory_space=pltpu.VMEM)
    return pl.pallas_call(
        score_kernel,
        out_shape=(
            jax.ShapeDtypeStruct((32, 256, 128), jnp.float32),
            jax.ShapeDtypeStruct((16, 8, 256), jnp.float32),
        ),
        in_specs=[vmem, vmem, vmem],
        out_specs=(vmem, vmem),
        scratch_shapes=[pltpu.VMEM((32, 256, 128), jnp.float32)],
        compiler_params=limit(24),
        cost_estimate=cost(8),
    )(asked, count, slab)


def pull_kernel(place_ref, stat_ref, weight_ref, share_ref, slab_ref, out_ref, factor, total):
    step = pl.program_id(0)

    @pl.when(step == 0)
    def _():
        stats = stat_ref[...]
        tops, masses = stats[:, 0], stats[:, 1]
        best = jnp.max(tops, axis=0, keepdims=True)
        mass = jnp.sum(jnp.exp(tops - best) * masses, axis=0, keepdims=True)
        mine = stat_ref[place_ref[2]][0:1]
        line = loss_scale * jnp.exp(mine - best) / mass
        factor[...] = jnp.transpose(jnp.broadcast_to(line, (128, 256)))
        total[...] = jnp.zeros_like(total)

    coef = jnp.concatenate(
        [weight_ref[i] * factor[...] - loss_scale * share_ref[i] for i in range(4)], axis=1
    )
    both = jnp.concatenate(halves(coef), axis=0)
    got = jnp.dot(both, slab_ref[...], preferred_element_type=jnp.float32)
    total[...] += got[:256] + got[256:]

    @pl.when(step == 7)
    def _():
        out_ref[...] = total[...].astype(jnp.bfloat16)


def pull(place, stats, weight, share, slab):
    quarter = pl.BlockSpec((4, 256, 128), lambda j, place: (j, 0, 0))
    return pl.pallas_call(
        pull_kernel,
        grid_spec=pltpu.PrefetchScalarGridSpec(
            num_scalar_prefetch=1,
            grid=(8,),
            in_specs=[whole(16, 8, 256), quarter, quarter, pl.BlockSpec((512, 768), lambda j, place: (j, 0))],
            out_specs=whole(256, 768),
            scratch_shapes=[pltpu.VMEM((256, 128), jnp.float32), pltpu.VMEM((256, 768), jnp.float32)],
        ),
        out_shape=jax.ShapeDtypeStruct((256, 768), jnp.bfloat16),
        compiler_params=limit(16),
        cost_estimate=cost(5),
    )(place, stats, weight, share, slab)


def resid_kernel(came_ref, normed_ref, rstd_ref, vectors_ref, resid_grad_ref, out_grad_ref, ups):
    step = pl.program_id(0)

    @pl.when(step == 0)
    def _():
        ups[...] = jnp.sum(came_ref[...].astype(jnp.float32), axis=0) * (1 / 64) * vectors_ref[:, 768:1536]

    for q in range(4):
        up = ups[pl.ds(step * 4 + q, 1), :]
        rows = slice(q * 64, q * 64 + 64)
        normed = normed_ref[rows, :]
        along = jnp.mean(up * normed, axis=-1, keepdims=True)
        grad = (up - jnp.mean(up, axis=-1, keepdims=True) - normed * along) * rstd_ref[rows, :]
        resid_grad_ref[rows, :] = grad
        out_grad_ref[rows, :] = grad.astype(jnp.bfloat16)


def resid_gradient(came, normed, rstd, vectors):
    rows = pl.BlockSpec((256, 768), lambda j: (j, 0))
    return pl.pallas_call(
        resid_kernel,
        grid=(4,),
        in_specs=[
            whole(16, 16, 768),
            rows,
            pl.BlockSpec((256, 1), lambda j: (j, 0)),
            whole(1, 3072),
        ],
        out_specs=(rows, rows),
        out_shape=(
            jax.ShapeDtypeStruct((1024, 768), jnp.float32),
            jax.ShapeDtypeStruct((1024, 768), jnp.bfloat16),
        ),
        scratch_shapes=[pltpu.VMEM((16, 768), jnp.float32)],
        compiler_params=limit(16),
        cost_estimate=cost(2),
    )(came, normed, rstd, vectors)


def weight_kernel(place_ref, left_ref, right_ref, away_ref, kept_ref):
    got = columns_dot(left_ref[...], right_ref[...])
    core = place_ref[0]
    for mine in range(2):

        @pl.when(core == mine)
        def _():
            kept_ref[0] = got[mine * 384 : mine * 384 + 384].astype(jnp.bfloat16)
            away_ref[0] = got[384 - mine * 384 : 768 - mine * 384].astype(jnp.bfloat16)


def weight_sums(place, left, right):
    return pl.pallas_call(
        weight_kernel,
        grid_spec=pltpu.PrefetchScalarGridSpec(
            num_scalar_prefetch=1,
            grid=(4,),
            in_specs=[pl.BlockSpec((1024, 768), lambda j, place: (0, j)), whole(1024, 768)],
            out_specs=(pl.BlockSpec((1, 384, 768), lambda j, place: (j, 0, 0)),) * 2,
        ),
        out_shape=(jax.ShapeDtypeStruct((4, 384, 768), jnp.bfloat16),) * 2,
        compiler_params=limit(24),
        cost_estimate=cost(40),
    )(place, left, right)


def second_kernel(place_ref, kept_ref, came_ref, carry_ref, own_ref, one_ref, three_ref, two_ref, carried_ref):
    for out, step in ((own_ref, 0), (one_ref, 1), (three_ref, 3), (two_ref, 2)):
        at = (place_ref[1] + step) % 4
        out[...] = (kept_ref[at].astype(jnp.float32) + came_ref[at].astype(jnp.float32)).astype(out.dtype)


def second_pair(place, kept, came, carry):
    block = lambda j, place: (0, j, 0)
    piece = pl.BlockSpec((96, 768), lambda j, place: (j, 0))
    return pl.pallas_call(
        second_kernel,
        grid_spec=pltpu.PrefetchScalarGridSpec(
            num_scalar_prefetch=1,
            grid=(4,),
            in_specs=[pl.BlockSpec((4, 96, 768), block), pl.BlockSpec((4, 96, 768), block), anywhere],
            out_specs=(piece,) * 4 + (anywhere,),
        ),
        out_shape=(jax.ShapeDtypeStruct((384, 768), jnp.float32),)
        + (jax.ShapeDtypeStruct((384, 768), jnp.bfloat16),) * 3
        + (jax.ShapeDtypeStruct(carry.shape, carry.dtype),),
        input_output_aliases={3: 4},
        compiler_params=limit(16),
        cost_estimate=cost(5),
    )(place, kept, came, carry)


def first_kernel(place_ref, kept_ref, came_ref, *refs):
    own_ref, one_ref, three_ref, two_ref, right_ref = refs[-6:-1]
    for out, step in ((own_ref, 0), (one_ref, 1), (three_ref, 3), (two_ref, 2)):
        at = (place_ref[1] + step) % 4
        got = kept_ref[at, :, :384].astype(jnp.float32) + came_ref[at, :, :384].astype(jnp.float32)
        out[...] = got.astype(out.dtype)
    right = [
        kept_ref[y, :, 384:].astype(jnp.float32) + came_ref[y, :, 384:].astype(jnp.float32) for y in range(4)
    ]
    for i in range(4):
        rows = slice(i * 24, i * 24 + 24)
        right_ref[i] = jnp.concatenate([part[rows] for part in right], axis=0).astype(jnp.bfloat16)


def first_pair(place, kept, came, carry, *after):
    block = lambda j, place: (0, j, 0)
    piece = pl.BlockSpec((96, 384), lambda j, place: (j, 0))
    return pl.pallas_call(
        first_kernel,
        grid_spec=pltpu.PrefetchScalarGridSpec(
            num_scalar_prefetch=1,
            grid=(4,),
            in_specs=[pl.BlockSpec((4, 96, 768), block), pl.BlockSpec((4, 96, 768), block)]
            + [anywhere] * (1 + len(after)),
            out_specs=(piece,) * 4 + (pl.BlockSpec((4, 96, 384), lambda j, place: (j, 0, 0)), anywhere),
        ),
        out_shape=(jax.ShapeDtypeStruct((384, 384), jnp.float32),)
        + (jax.ShapeDtypeStruct((384, 384), jnp.bfloat16),) * 3
        + (
            jax.ShapeDtypeStruct((16, 96, 384), jnp.bfloat16),
            jax.ShapeDtypeStruct(carry.shape, carry.dtype),
        ),
        input_output_aliases={3: 5},
        compiler_params=limit(56),
        cost_estimate=cost(5),
    )(place, kept, came, carry, *after)


def hold(carry, *after):
    return pl.pallas_call(
        lambda *refs: None,
        in_specs=[anywhere] * (1 + len(after)),
        out_specs=anywhere,
        out_shape=jax.ShapeDtypeStruct(carry.shape, carry.dtype),
        input_output_aliases={0: 0},
        compiler_params=limit(4),
        cost_estimate=cost(1),
    )(carry, *after)


def mark_kernel(own_ref, out_ref):
    out_ref[...] = own_ref[...]


def mark(own):
    tile = pl.BlockSpec((8, 128), lambda j: (0, 0))
    return pl.pallas_call(
        mark_kernel,
        grid=(1,),
        in_specs=[tile],
        out_specs=tile,
        out_shape=jax.ShapeDtypeStruct((8, 128), jnp.float32),
        compiler_params=limit(4),
        cost_estimate=cost(100),
    )(own)


def left_kernel(*refs):
    out_ref = refs[-1]
    for parts, cols in ((refs[:4], slice(0, 384)), (refs[4:8], slice(384, 1152))):
        total = parts[0][...]
        for part in parts[1:]:
            total = total + part[...].astype(jnp.float32)
        out_ref[:, cols] = total.astype(jnp.bfloat16)


def left_sums(first, second, after):
    narrow, wide = (pl.BlockSpec((192, n), lambda j: (j, 0)) for n in (384, 768))
    return pl.pallas_call(
        left_kernel,
        grid=(2,),
        in_specs=[narrow] * 4 + [wide] * 4 + [anywhere],
        out_specs=pl.BlockSpec((192, 1152), lambda j: (j, 0)),
        out_shape=jax.ShapeDtypeStruct((384, 1152), jnp.bfloat16),
        compiler_params=limit(16),
        cost_estimate=cost(2),
    )(*first, *second, after)


def right_kernel(y_ref, came_ref, after_ref, own_ref, one_ref, three_ref, two_ref, total):
    total[...] = jnp.sum(came_ref[...].astype(jnp.float32), axis=0)
    for out, step in ((own_ref, 0), (one_ref, 1), (three_ref, 3), (two_ref, 2)):
        at = (y_ref[0] + step) % 4
        out[...] = total[pl.ds(pl.multiple_of(at * 24, 8), 24), :]


def right_sums(y, came, after):
    vmem = pl.BlockSpec(memory_space=pltpu.VMEM)
    return pl.pallas_call(
        right_kernel,
        in_specs=[pl.BlockSpec(memory_space=pltpu.SMEM), vmem, anywhere],
        out_specs=(vmem,) * 4,
        out_shape=(jax.ShapeDtypeStruct((24, 384), jnp.float32),) * 4,
        scratch_shapes=[pltpu.VMEM((96, 384), jnp.float32)],
        compiler_params=limit(8),
        cost_estimate=cost(1),
    )(y, came, after)


def last_kernel(devices, left_ref, own_ref, one_ref, three_ref, two_ref, out_ref):
    left = jnp.sum(left_ref[...].astype(jnp.float32), axis=0) / devices
    right = (own_ref[...] + one_ref[...] + three_ref[...] + two_ref[...]) / devices
    out_ref[:, :384] = left[:, :384]
    out_ref[:, 384:768] = right
    out_ref[:, 768:] = left[:, 384:]


def last_sums(devices, left, *right):
    vmem = pl.BlockSpec(memory_space=pltpu.VMEM)
    return pl.pallas_call(
        lambda *refs: last_kernel(devices, *refs),
        in_specs=[vmem] * 5,
        out_specs=vmem,
        out_shape=jax.ShapeDtypeStruct((24, 1536), jnp.float32),
        compiler_params=limit(8),
        cost_estimate=cost(1),
    )(left, *right)


def body(
    tokens, w_in, bias_in, w_out, bias_out, gain, shift, slab, owners, offsets, reader_weights
):
    devices = lax.axis_size("query") * lax.axis_size("index")
    me = lax.axis_index("index")[None]
    y = lax.axis_index("query") // 2
    core = lax.axis_index("query") % 2
    place = jnp.stack([core, y, me[0]])

    asked = exchange(table(owners[..., 0], offsets, reader_weights))
    vectors = jnp.concatenate([bias_out, gain, shift, jnp.zeros_like(shift)]).reshape(1, 3072)
    hidden, slopes, normed, rstd, ask = forward(tokens, w_in, bias_in, w_out, vectors)
    count, share = picks(place, asked, rstd)
    weight, stat = score(exchange(ask), count, slab)
    partial = pull(place, exchange(stat), weight, share, slab)
    came = exchange(partial.reshape(16, 16, 768))
    resid_grad, out_grad = resid_gradient(came, normed, rstd, vectors)

    def round_y(own, *pieces):
        return [own] + [shifted(piece, 0, step) for piece, step in zip(pieces, (1, 3, 2))]

    away, kept = weight_sums(place, hidden, out_grad)
    *second, out_grad = second_pair(place, kept, shifted(away, 1, 0), out_grad)
    second = round_y(*second)
    pre_grad = (
        jnp.dot(out_grad, w_out.T, preferred_element_type=jnp.float32) * slopes.astype(jnp.float32)
    ).astype(jnp.bfloat16)
    away, kept = weight_sums(place, pre_grad, tokens)
    away = hold(away, second[1], second[2])
    *first, packed, pre_grad = first_pair(
        place, kept, shifted(away, 1, 0), pre_grad, mark(second[0])
    )
    first = round_y(*first)
    right = exchange(packed)
    token_grads = (
        resid_grad + jnp.dot(pre_grad, w_in.T, preferred_element_type=jnp.float32)
    ).astype(jnp.bfloat16)

    left = exchange(left_sums(first, second, token_grads).reshape(16, 24, 1152))
    own, one, three, two = right_sums(y[None], right, token_grads)
    right = round_y(own, one, three, two)
    return (token_grads, last_sums(devices, left, *right))


def solution(mesh):
    placed = (
        P(("query", "index"), None),
        P(),
        P(),
        P(),
        P(),
        P(),
        P(),
        P("index", None),
        P(("query", "index"), None, None),
        P(("query", "index"), None),
        P(("query", "index"), None),
    )
    return jax.shard_map(
        body,
        mesh=mesh,
        in_specs=placed,
        out_specs=(P(("query", "index"), None), P(("query", "index"), None)),
        check_vma=False,
    )
```

```python
import jax
import jax.numpy as jnp
from jax import lax
from jax.experimental import pallas as pl
from jax.experimental.pallas import tpu as pltpu
from jax.sharding import PartitionSpec as P

loss_scale = 256.0
norm_eps = 1e-12
every = ("query", "index")
MIB = 1 << 20
low = -1e30


def limit(mib):
    return pltpu.CompilerParams(vmem_limit_bytes=mib * MIB)


def cost(us):
    return pl.CostEstimate(flops=us * 1_000_000_000, bytes_accessed=1000, transcendentals=0)
anywhere = pl.BlockSpec(memory_space=pl.ANY)


def halves(value):
    first = value.astype(jnp.bfloat16)
    return first, (value - first.astype(jnp.float32)).astype(jnp.bfloat16)


def dot_rows(left, right):
    return lax.dot_general(left, right, (((1,), (1,)), ((), ())), preferred_element_type=jnp.float32)


def columns_dot(left, right):
    return lax.dot_general(left, right, (((0,), (0,)), ((), ())), preferred_element_type=jnp.float32)


def exchange(value):
    return lax.all_to_all(value, "index", 0, 0, tiled=True)


def shifted(value, core, along_y):
    pairs = []
    for query in range(8):
        y, c = query // 2, query % 2
        to = ((y + along_y) % 4) * 2 + (c + core) % 2
        pairs += [(query * 16 + i, to * 16 + i) for i in range(16)]
    return lax.ppermute(value, every, pairs)


def whole(*shape):
    return pl.BlockSpec(shape, lambda *_: (0,) * len(shape))


def slope(pre):
    square = pre * pre
    bend = jnp.tanh(pre * (0.7978845608028654 + 0.035677408136300125 * square))
    share = 0.5 + 0.5 * bend
    value = pre * share
    grad = share + (value - value * share) * (1.5957691216057308 + 0.21406444881780074 * square)
    return value, grad


def forward_kernel(
    tokens_ref, w_in_ref, bias_in_ref, w_out_ref, vectors_ref,
    hidden_ref, slope_ref, normed_ref, rstd_ref, ask_ref, resid, query, pres,
):
    step = pl.program_id(0)

    @pl.when(step == 0)
    def _():
        resid[...] = tokens_ref[...].astype(jnp.float32) + vectors_ref[:, :768]

    for part in range(10):
        if part < 8:
            rows = slice(part * 128, part * 128 + 128)
            pres[rows, :] = jnp.dot(tokens_ref[rows, :], w_in_ref[...], preferred_element_type=jnp.float32)
        if 1 <= part < 9:
            for start in range(part * 128 - 128, part * 128, 16):
                rows = slice(start, start + 16)
                value, grad = slope(pres[rows, :] + bias_in_ref[...])
                hidden_ref[rows, :] = value.astype(jnp.bfloat16)
                slope_ref[rows, :] = grad.astype(jnp.bfloat16)
        if 2 <= part:
            rows = slice(part * 128 - 256, part * 128 - 128)
            resid[rows, :] += jnp.dot(hidden_ref[rows, :], w_out_ref[...], preferred_element_type=jnp.float32)

    @pl.when(step == pl.num_programs(0) - 1)
    def _():
        for q in range(16):
            rows = slice(q * 64, q * 64 + 64)
            here = resid[rows, :]
            away = here - jnp.mean(here, axis=-1, keepdims=True)
            rstd = lax.rsqrt(jnp.mean(away * away, axis=-1, keepdims=True) + norm_eps)
            normed = away * rstd
            normed_ref[rows, :] = normed
            rstd_ref[rows, :] = rstd
            query[q : q + 1, :] = (
                jnp.sum(normed, axis=0, keepdims=True) * (1 / 64) * vectors_ref[:, 768:1536] + vectors_ref[:, 1536:2304]
            )
        upper, lower = halves(query[...])
        for to in range(16):
            ask_ref[to, :, :768] = upper
            ask_ref[to, :, 768:] = lower


def forward(tokens, w_in, bias_in, w_out, vectors):
    block = 512
    units = pl.BlockSpec((1024, block), lambda j: (0, j))
    return pl.pallas_call(
        forward_kernel,
        grid=(3072 // block,),
        in_specs=[
            whole(1024, 768),
            pl.BlockSpec((768, block), lambda j: (0, j)),
            pl.BlockSpec((1, block), lambda j: (0, j)),
            pl.BlockSpec((block, 768), lambda j: (j, 0)),
            whole(1, 3072),
        ],
        out_specs=(units, units, whole(1024, 768), whole(1024, 1), whole(16, 16, 1536)),
        out_shape=(
            jax.ShapeDtypeStruct((1024, 3072), jnp.bfloat16),
            jax.ShapeDtypeStruct((1024, 3072), jnp.bfloat16),
            jax.ShapeDtypeStruct((1024, 768), jnp.float32),
            jax.ShapeDtypeStruct((1024, 1), jnp.float32),
            jax.ShapeDtypeStruct((16, 16, 1536), jnp.bfloat16),
        ),
        scratch_shapes=[
            pltpu.VMEM((1024, 768), jnp.float32),
            pltpu.VMEM((16, 768), jnp.float32),
            pltpu.VMEM((1024, block), jnp.float32),
        ],
        compiler_params=limit(56),
        cost_estimate=cost(20),
    )(tokens, w_in, bias_in.reshape(1, -1), w_out, vectors)


def table_kernel(owner_ref, offset_ref, weight_ref, out_ref):
    weight = weight_ref[...]
    target = weight / jnp.sum(weight, axis=-1, keepdims=True)
    offset = offset_ref[...]
    upper, lower = halves(target)
    fields = [
        owner_ref[...].astype(jnp.float32),
        (offset // 128).astype(jnp.float32),
        (offset % 128).astype(jnp.float32),
        upper.astype(jnp.float32),
        lower.astype(jnp.float32),
    ]
    rows = [
        jnp.concatenate([field[g * 8 + i : g * 8 + i + 1] for i in range(8)], axis=1)
        for field in fields
        for g in range(2)
    ]
    rows = jnp.concatenate(rows + [jnp.zeros((6, 512), jnp.float32)], axis=0).astype(jnp.bfloat16)
    for to in range(16):
        out_ref[to] = rows


def table(owners, offsets, reader_weights):
    vmem = pl.BlockSpec(memory_space=pltpu.VMEM)
    return pl.pallas_call(
        table_kernel,
        in_specs=[vmem] * 3,
        out_specs=vmem,
        out_shape=jax.ShapeDtypeStruct((16, 16, 512), jnp.bfloat16),
        compiler_params=limit(56),
        cost_estimate=cost(1),
    )(owners, offsets, reader_weights)


def picks_kernel(place_ref, table_ref, after_ref, count_ref, share_ref):
    me = place_ref[2].astype(jnp.float32)
    turn = (lax.broadcasted_iota(jnp.int32, (1, 512), 1) // 64).astype(jnp.float32)
    row = lax.broadcasted_iota(jnp.int32, (256, 512), 0).astype(jnp.float32)
    line = lax.broadcasted_iota(jnp.int32, (128, 512), 0).astype(jnp.float32)

    def source(s, carry):
        meta = table_ref[s].astype(jnp.float32)
        counts = []
        for g in range(2):
            owner, high, spot, upper, lower = [meta[2 * f + g : 2 * f + g + 1] for f in range(5)]
            key = jnp.where(owner == me, high * 8.0 + turn, -1.0)
            left = jnp.where(row == key, 1.0, 0.0).astype(jnp.bfloat16)
            hit = line == spot
            right = jnp.concatenate(
                [jnp.where(hit, 1.0, 0.0), jnp.where(hit, upper, 0.0), jnp.where(hit, lower, 0.0)], axis=0
            ).astype(jnp.bfloat16)
            out = dot_rows(left, right)
            at = pl.ds(pl.multiple_of(s * 16 + g * 8, 8), 8)
            counts.append(out[:, :128].reshape(32, 8, 128))
            share_ref[:, at, :] = (out[:, 128:256] + out[:, 256:]).reshape(32, 8, 128)
        at = pl.ds(pl.multiple_of(s * 16, 16), 16)
        count_ref[:, at, :] = jnp.concatenate(counts, axis=1).astype(jnp.bfloat16)
        return carry

    lax.fori_loop(0, 16, source, 0, unroll=2)


def picks(place, asked, after):
    vmem = pl.BlockSpec(memory_space=pltpu.VMEM)
    return pl.pallas_call(
        picks_kernel,
        out_shape=(
            jax.ShapeDtypeStruct((32, 256, 128), jnp.bfloat16),
            jax.ShapeDtypeStruct((32, 256, 128), jnp.float32),
        ),
        in_specs=[pl.BlockSpec(memory_space=pltpu.SMEM), vmem, anywhere],
        out_specs=(vmem, vmem),
        compiler_params=limit(24),
        cost_estimate=cost(10),
    )(place, asked, after)


def score_kernel(ask_ref, count_ref, slab, weight_ref, stat_ref, scores):
    both = jnp.concatenate(
        [ask_ref[:, :, :768].reshape(256, 768), ask_ref[:, :, 768:].reshape(256, 768)], axis=0
    )
    top = jnp.full((256, 128), low, jnp.float32)
    for block in range(8):
        got = dot_rows(both, slab[block * 512 : block * 512 + 512])
        got = got[:256] + got[256:]
        for i in range(4):
            part = got[:, i * 128 : i * 128 + 128]
            scores[block * 4 + i] = part
            top = jnp.maximum(top, jnp.where(count_ref[block * 4 + i].astype(jnp.float32) > 0, part, low))
    top = jnp.max(top, axis=1, keepdims=True)
    mass = jnp.zeros((256, 128), jnp.float32)
    for high in range(32):
        here = count_ref[high].astype(jnp.float32)
        part = jnp.where(here > 0, here * jnp.exp(jnp.minimum(scores[high] - top, 0.0)), 0.0)
        mass = mass + part
        weight_ref[high] = part
    mass = jnp.sum(mass, axis=1, keepdims=True)
    lane = lax.broadcasted_iota(jnp.int32, (256, 128), 1)
    stat = jnp.transpose(jnp.where(lane == 0, top, mass))[:8]
    for to in range(16):
        stat_ref[to] = stat


def score(asked, count, slab):
    vmem = pl.BlockSpec(memory_space=pltpu.VMEM)
    return pl.pallas_call(
        score_kernel,
        out_shape=(
            jax.ShapeDtypeStruct((32, 256, 128), jnp.float32),
            jax.ShapeDtypeStruct((16, 8, 256), jnp.float32),
        ),
        in_specs=[vmem, vmem, vmem],
        out_specs=(vmem, vmem),
        scratch_shapes=[pltpu.VMEM((32, 256, 128), jnp.float32)],
        compiler_params=limit(24),
        cost_estimate=cost(8),
    )(asked, count, slab)


def pull_kernel(place_ref, stat_ref, weight_ref, share_ref, slab_ref, out_ref, factor, total):
    step = pl.program_id(0)

    @pl.when(step == 0)
    def _():
        stats = stat_ref[...]
        tops, masses = stats[:, 0], stats[:, 1]
        best = jnp.max(tops, axis=0, keepdims=True)
        mass = jnp.sum(jnp.exp(tops - best) * masses, axis=0, keepdims=True)
        mine = stat_ref[place_ref[2]][0:1]
        line = loss_scale * jnp.exp(mine - best) / mass
        factor[...] = jnp.transpose(jnp.broadcast_to(line, (128, 256)))
        total[...] = jnp.zeros_like(total)

    coef = jnp.concatenate(
        [weight_ref[i] * factor[...] - loss_scale * share_ref[i] for i in range(4)], axis=1
    )
    both = jnp.concatenate(halves(coef), axis=0)
    got = jnp.dot(both, slab_ref[...], preferred_element_type=jnp.float32)
    total[...] += got[:256] + got[256:]

    @pl.when(step == 7)
    def _():
        out_ref[...] = total[...].astype(jnp.bfloat16)


def pull(place, stats, weight, share, slab):
    quarter = pl.BlockSpec((4, 256, 128), lambda j, place: (j, 0, 0))
    return pl.pallas_call(
        pull_kernel,
        grid_spec=pltpu.PrefetchScalarGridSpec(
            num_scalar_prefetch=1,
            grid=(8,),
            in_specs=[whole(16, 8, 256), quarter, quarter, pl.BlockSpec((512, 768), lambda j, place: (j, 0))],
            out_specs=whole(256, 768),
            scratch_shapes=[pltpu.VMEM((256, 128), jnp.float32), pltpu.VMEM((256, 768), jnp.float32)],
        ),
        out_shape=jax.ShapeDtypeStruct((256, 768), jnp.bfloat16),
        compiler_params=limit(16),
        cost_estimate=cost(5),
    )(place, stats, weight, share, slab)


def resid_kernel(came_ref, normed_ref, rstd_ref, vectors_ref, resid_grad_ref, out_grad_ref, ups):
    step = pl.program_id(0)

    @pl.when(step == 0)
    def _():
        ups[...] = jnp.sum(came_ref[...].astype(jnp.float32), axis=0) * (1 / 64) * vectors_ref[:, 768:1536]

    for q in range(4):
        up = ups[pl.ds(step * 4 + q, 1), :]
        rows = slice(q * 64, q * 64 + 64)
        normed = normed_ref[rows, :]
        along = jnp.mean(up * normed, axis=-1, keepdims=True)
        grad = (up - jnp.mean(up, axis=-1, keepdims=True) - normed * along) * rstd_ref[rows, :]
        resid_grad_ref[rows, :] = grad
        out_grad_ref[rows, :] = grad.astype(jnp.bfloat16)


def resid_gradient(came, normed, rstd, vectors):
    rows = pl.BlockSpec((256, 768), lambda j: (j, 0))
    return pl.pallas_call(
        resid_kernel,
        grid=(4,),
        in_specs=[
            whole(16, 16, 768),
            rows,
            pl.BlockSpec((256, 1), lambda j: (j, 0)),
            whole(1, 3072),
        ],
        out_specs=(rows, rows),
        out_shape=(
            jax.ShapeDtypeStruct((1024, 768), jnp.float32),
            jax.ShapeDtypeStruct((1024, 768), jnp.bfloat16),
        ),
        scratch_shapes=[pltpu.VMEM((16, 768), jnp.float32)],
        compiler_params=limit(16),
        cost_estimate=cost(2),
    )(came, normed, rstd, vectors)


def weight_kernel(place_ref, left_ref, right_ref, away_ref, kept_ref):
    got = columns_dot(left_ref[...], right_ref[...])
    core = place_ref[0]
    for mine in range(2):

        @pl.when(core == mine)
        def _():
            kept_ref[0] = got[mine * 384 : mine * 384 + 384].astype(jnp.bfloat16)
            away_ref[0] = got[384 - mine * 384 : 768 - mine * 384].astype(jnp.bfloat16)


def weight_sums(place, left, right):
    return pl.pallas_call(
        weight_kernel,
        grid_spec=pltpu.PrefetchScalarGridSpec(
            num_scalar_prefetch=1,
            grid=(4,),
            in_specs=[pl.BlockSpec((1024, 768), lambda j, place: (0, j)), whole(1024, 768)],
            out_specs=(pl.BlockSpec((1, 384, 768), lambda j, place: (j, 0, 0)),) * 2,
        ),
        out_shape=(jax.ShapeDtypeStruct((4, 384, 768), jnp.bfloat16),) * 2,
        compiler_params=limit(24),
        cost_estimate=cost(40),
    )(place, left, right)


def half_kernel(place_ref, left_ref, right_ref, out_ref):
    out_ref[0] = columns_dot(left_ref[...], right_ref[...]).astype(jnp.bfloat16)


def weight_half(place, left, right, other):
    def units(j, place):
        return 0, 2 * j + (1 - place[0] if other else place[0])

    return pl.pallas_call(
        half_kernel,
        grid_spec=pltpu.PrefetchScalarGridSpec(
            num_scalar_prefetch=1,
            grid=(4,),
            in_specs=[pl.BlockSpec((1024, 384), units), whole(1024, 768)],
            out_specs=pl.BlockSpec((1, 384, 768), lambda j, place: (j, 0, 0)),
        ),
        out_shape=jax.ShapeDtypeStruct((4, 384, 768), jnp.bfloat16),
        compiler_params=limit(24),
        cost_estimate=cost(40),
    )(place, left, right)


def second_kernel(place_ref, kept_ref, came_ref, carry_ref, own_ref, one_ref, three_ref, two_ref, carried_ref):
    for out, step in ((own_ref, 0), (one_ref, 1), (three_ref, 3), (two_ref, 2)):
        at = (place_ref[1] + step) % 4
        out[...] = (kept_ref[at].astype(jnp.float32) + came_ref[at].astype(jnp.float32)).astype(out.dtype)


def second_pair(place, kept, came, carry):
    block = lambda j, place: (0, j, 0)
    piece = pl.BlockSpec((96, 768), lambda j, place: (j, 0))
    return pl.pallas_call(
        second_kernel,
        grid_spec=pltpu.PrefetchScalarGridSpec(
            num_scalar_prefetch=1,
            grid=(4,),
            in_specs=[pl.BlockSpec((4, 96, 768), block), pl.BlockSpec((4, 96, 768), block), anywhere],
            out_specs=(piece,) * 4 + (anywhere,),
        ),
        out_shape=(jax.ShapeDtypeStruct((384, 768), jnp.float32),)
        + (jax.ShapeDtypeStruct((384, 768), jnp.bfloat16),) * 3
        + (jax.ShapeDtypeStruct(carry.shape, carry.dtype),),
        input_output_aliases={3: 4},
        compiler_params=limit(16),
        cost_estimate=cost(5),
    )(place, kept, came, carry)


def first_kernel(place_ref, kept_ref, came_ref, *refs):
    own_ref, one_ref, three_ref, two_ref, right_ref = refs[-6:-1]
    for out, step in ((own_ref, 0), (one_ref, 1), (three_ref, 3), (two_ref, 2)):
        at = (place_ref[1] + step) % 4
        got = kept_ref[at, :, :384].astype(jnp.float32) + came_ref[at, :, :384].astype(jnp.float32)
        out[...] = got.astype(out.dtype)
    right = [
        kept_ref[y, :, 384:].astype(jnp.float32) + came_ref[y, :, 384:].astype(jnp.float32) for y in range(4)
    ]
    for i in range(4):
        rows = slice(i * 24, i * 24 + 24)
        right_ref[i] = jnp.concatenate([part[rows] for part in right], axis=0).astype(jnp.bfloat16)


def first_pair(place, kept, came, carry, *after):
    block = lambda j, place: (0, j, 0)
    piece = pl.BlockSpec((96, 384), lambda j, place: (j, 0))
    return pl.pallas_call(
        first_kernel,
        grid_spec=pltpu.PrefetchScalarGridSpec(
            num_scalar_prefetch=1,
            grid=(4,),
            in_specs=[pl.BlockSpec((4, 96, 768), block), pl.BlockSpec((4, 96, 768), block)]
            + [anywhere] * (1 + len(after)),
            out_specs=(piece,) * 4 + (pl.BlockSpec((4, 96, 384), lambda j, place: (j, 0, 0)), anywhere),
        ),
        out_shape=(jax.ShapeDtypeStruct((384, 384), jnp.float32),)
        + (jax.ShapeDtypeStruct((384, 384), jnp.bfloat16),) * 3
        + (
            jax.ShapeDtypeStruct((16, 96, 384), jnp.bfloat16),
            jax.ShapeDtypeStruct(carry.shape, carry.dtype),
        ),
        input_output_aliases={3: 5},
        compiler_params=limit(56),
        cost_estimate=cost(5),
    )(place, kept, came, carry, *after)


def hold(carry, *after):
    return pl.pallas_call(
        lambda *refs: None,
        in_specs=[anywhere] * (1 + len(after)),
        out_specs=anywhere,
        out_shape=jax.ShapeDtypeStruct(carry.shape, carry.dtype),
        input_output_aliases={0: 0},
        compiler_params=limit(4),
        cost_estimate=cost(1),
    )(carry, *after)


def mark_kernel(own_ref, out_ref):
    out_ref[...] = own_ref[...]


def mark(own):
    tile = pl.BlockSpec((8, 128), lambda j: (0, 0))
    return pl.pallas_call(
        mark_kernel,
        grid=(1,),
        in_specs=[tile],
        out_specs=tile,
        out_shape=jax.ShapeDtypeStruct((8, 128), jnp.float32),
        compiler_params=limit(4),
        cost_estimate=cost(100),
    )(own)


def left_kernel(*refs):
    out_ref = refs[-1]
    for parts, cols in ((refs[:4], slice(0, 384)), (refs[4:8], slice(384, 1152))):
        total = parts[0][...]
        for part in parts[1:]:
            total = total + part[...].astype(jnp.float32)
        out_ref[:, cols] = total.astype(jnp.bfloat16)


def left_sums(first, second, after):
    narrow, wide = (pl.BlockSpec((192, n), lambda j: (j, 0)) for n in (384, 768))
    return pl.pallas_call(
        left_kernel,
        grid=(2,),
        in_specs=[narrow] * 4 + [wide] * 4 + [anywhere],
        out_specs=pl.BlockSpec((192, 1152), lambda j: (j, 0)),
        out_shape=jax.ShapeDtypeStruct((384, 1152), jnp.bfloat16),
        compiler_params=limit(16),
        cost_estimate=cost(2),
    )(*first, *second, after)


def right_kernel(y_ref, came_ref, after_ref, own_ref, one_ref, three_ref, two_ref, total):
    total[...] = jnp.sum(came_ref[...].astype(jnp.float32), axis=0)
    for out, step in ((own_ref, 0), (one_ref, 1), (three_ref, 3), (two_ref, 2)):
        at = (y_ref[0] + step) % 4
        out[...] = total[pl.ds(pl.multiple_of(at * 24, 8), 24), :]


def right_sums(y, came, after):
    vmem = pl.BlockSpec(memory_space=pltpu.VMEM)
    return pl.pallas_call(
        right_kernel,
        in_specs=[pl.BlockSpec(memory_space=pltpu.SMEM), vmem, anywhere],
        out_specs=(vmem,) * 4,
        out_shape=(jax.ShapeDtypeStruct((24, 384), jnp.float32),) * 4,
        scratch_shapes=[pltpu.VMEM((96, 384), jnp.float32)],
        compiler_params=limit(8),
        cost_estimate=cost(1),
    )(y, came, after)


def last_kernel(devices, left_ref, own_ref, one_ref, three_ref, two_ref, out_ref):
    left = jnp.sum(left_ref[...].astype(jnp.float32), axis=0) / devices
    right = (own_ref[...] + one_ref[...] + three_ref[...] + two_ref[...]) / devices
    out_ref[:, :384] = left[:, :384]
    out_ref[:, 384:768] = right
    out_ref[:, 768:] = left[:, 384:]


def last_sums(devices, left, *right):
    vmem = pl.BlockSpec(memory_space=pltpu.VMEM)
    return pl.pallas_call(
        lambda *refs: last_kernel(devices, *refs),
        in_specs=[vmem] * 5,
        out_specs=vmem,
        out_shape=jax.ShapeDtypeStruct((24, 1536), jnp.float32),
        compiler_params=limit(8),
        cost_estimate=cost(1),
    )(left, *right)


def body(
    tokens, w_in, bias_in, w_out, bias_out, gain, shift, slab, owners, offsets, reader_weights
):
    devices = lax.axis_size("query") * lax.axis_size("index")
    me = lax.axis_index("index")[None]
    y = lax.axis_index("query") // 2
    core = lax.axis_index("query") % 2
    place = jnp.stack([core, y, me[0]])

    asked = exchange(table(owners[..., 0], offsets, reader_weights))
    vectors = jnp.concatenate([bias_out, gain, shift, jnp.zeros_like(shift)]).reshape(1, 3072)
    hidden, slopes, normed, rstd, ask = forward(tokens, w_in, bias_in, w_out, vectors)
    count, share = picks(place, asked, rstd)
    weight, stat = score(exchange(ask), count, slab)
    partial = pull(place, exchange(stat), weight, share, slab)
    came = exchange(partial.reshape(16, 16, 768))
    resid_grad, out_grad = resid_gradient(came, normed, rstd, vectors)

    def round_y(own, *pieces):
        return [own] + [shifted(piece, 0, step) for piece, step in zip(pieces, (1, 3, 2))]

    away = weight_half(place, hidden, out_grad, True)
    kept = weight_half(place, hidden, out_grad, False)
    *second, out_grad = second_pair(place, kept, shifted(away, 1, 0), out_grad)
    second = round_y(*second)
    pre_grad = (
        jnp.dot(out_grad, w_out.T, preferred_element_type=jnp.float32) * slopes.astype(jnp.float32)
    ).astype(jnp.bfloat16)
    away, kept = weight_sums(place, pre_grad, tokens)
    away = hold(away, second[1], second[2])
    *first, packed, pre_grad = first_pair(
        place, kept, shifted(away, 1, 0), pre_grad, mark(second[0])
    )
    first = round_y(*first)
    right = exchange(packed)
    token_grads = (
        resid_grad + jnp.dot(pre_grad, w_in.T, preferred_element_type=jnp.float32)
    ).astype(jnp.bfloat16)

    left = exchange(left_sums(first, second, token_grads).reshape(16, 24, 1152))
    own, one, three, two = right_sums(y[None], right, token_grads)
    right = round_y(own, one, three, two)
    return (token_grads, last_sums(devices, left, *right))


def solution(mesh):
    placed = (
        P(("query", "index"), None),
        P(),
        P(),
        P(),
        P(),
        P(),
        P(),
        P("index", None),
        P(("query", "index"), None, None),
        P(("query", "index"), None),
        P(("query", "index"), None),
    )
    return jax.shard_map(
        body,
        mesh=mesh,
        in_specs=placed,
        out_specs=(P(("query", "index"), None), P(("query", "index"), None)),
        check_vma=False,
    )
```
